32 devices in a mesh: grp: 4 (over y, core), site: 8 (over z, x).
Axes of the slice: x: 2, y: 2, z: 4, core: 2. Of those that a mesh axis runs over, the one named last changes fastest.
Arguments:
- noise: bfloat16 [64, 4096], P(('grp', 'site')), may hold values from -25 to 25, as said below
- sites: bfloat16 [4096, 4096], P('site'), may hold values from -25 to 25, as said below
- weights: float32 [4096], P('site'), may hold values from -2 to 2
Outputs:
- targets: bfloat16 [64, 4096], P(('grp', 'site'))
- potentials: float32 [64], P(('grp', 'site'))
- new_weights: float32 [4096], P('site')
The draws below stay inside these ranges and needn't reach their ends.
Inputs may be any that keep to these rules, and one draw needn't show every extreme that they name: Entries of the noise rows are finite reals. Entries of the sites are finite reals.
All inputs are finite; a program needn't handle non-finite values.
Results may differ from the reference program's by a relative error of at most 0.014.
Values may be sent and summed in bfloat16 or wider, within the bound.
A program may use at most 64 MiB of HBM per device.

```python
import jax
import jax.numpy as jnp
from jax import lax

D = 4096
SITES = 4096
ROW_GRP = 16
ROWS = 64
N_GRP = 4


def draw_sites(key, part):
    values = jnp.clip(jax.random.normal(jax.random.fold_in(key, 1), (SITES, D), jnp.float32), -6.0, 6.0)
    return values.astype(jnp.bfloat16)


def draw_noise(key, part):
    values = jnp.clip(jax.random.normal(jax.random.fold_in(key, 2), (ROWS, D), jnp.float32), -6.0, 6.0)
    return values.astype(jnp.bfloat16)


def level_of(key, shape, cuts, smallest, top_value):
    factor_of = 1.0
    for axis_at, blocks in cuts:
        draws = jax.random.uniform(jax.random.fold_in(jax.random.fold_in(key, 6), axis_at), (blocks,), jnp.float32, smallest / len(cuts), top_value / len(cuts))
        factor_of = factor_of * jnp.repeat(jnp.exp(draws), shape[axis_at] // blocks).reshape((-1,) + (1,) * (len(shape) - 1 - axis_at))
    return factor_of


def scatter_about(rng, shape, width, reach, split=(), kind=jnp.bfloat16):
    drawn = jax.random.normal(rng, shape, jnp.float32) * width
    if len(split) > 0:
        drawn = level_of(rng, shape, split, -0.22, 0.18) * drawn
    return jnp.clip(drawn, min=-reach, max=reach).astype(kind)


def setup_inputs(seed: int = 0) -> dict:
    seeds = jax.random.split(jax.random.key(seed), 4)
    return {
        "noise": draw_noise(jax.random.fold_in(seeds[3], 71), 0),
        "sites": draw_sites(jax.random.fold_in(seeds[3], 71), 0),
        "weights": scatter_about(seeds[2], (SITES,), 0.5, 2.0, ((0, 8),), jnp.float32),
    }


EPS = 0.006
ETA = 0.05


def reference(noise, sites, weights):
    sites_f = sites.astype(jnp.float32)
    half_sq = jnp.sum(sites_f * sites_f, axis=1) / (2.0 * D)
    grouped = noise.reshape(N_GRP, ROW_GRP, D)

    def one_group(block):
        inner = jnp.dot(block, sites.T, preferred_element_type=jnp.float32)
        score = weights[None, :] + (inner / D - half_sq[None, :]) / EPS
        top = jnp.max(score, axis=1)
        lse = top + jnp.log(jnp.sum(jnp.exp(score - top[:, None]), axis=1))
        probs = jnp.exp(score - lse[:, None])
        probs_b = probs.astype(jnp.bfloat16)
        tgt = jnp.dot(probs_b, sites, preferred_element_type=jnp.float32).astype(jnp.bfloat16)
        block_f = block.astype(jnp.float32)
        pot = jnp.sum(block_f * block_f, axis=1) / (2.0 * D) - EPS * (lse - jnp.log(float(SITES)))
        return tgt, pot, jnp.sum(probs, axis=0)

    tgt, pot, mass_parts = lax.map(one_group, grouped)
    mass = jnp.sum(mass_parts, axis=0)
    new_weights = weights + ETA * (1.0 - (float(SITES) / float(ROWS)) * mass)
    return tgt.reshape(ROWS, D), pot.reshape(ROWS), new_weights
```

```python
import functools
import math

import jax
import jax.numpy as jnp
from jax import lax
from jax.experimental import pallas as pl
from jax.experimental.pallas import tpu as pltpu
from jax.sharding import PartitionSpec as P

EPS = 0.006
ETA = 0.05
MESH = pl.DeviceIdType.MESH
F32 = jnp.float32
BF16 = jnp.bfloat16


def steps(count, body):
    if count <= 16:
        for k in range(count):
            body(k)
    else:
        lax.fori_loop(0, count, lambda k, c: (body(k), c)[1], 0)


def kernel(n, g, noise_ref, sites_ref, weights_ref, tgt_ref, pot_ref, neww_ref,
           sites_v, noise_all, noise_f, sq_acc, t_full, t_send, t_all,
           stat_send, stat_all, mass_send, mass_all,
           site_sem, own_sem, ns_sem, nr_sem, ts_sem, tr_sem, ss_sem, sr_sem, ms_sem, mr_sem):
    me = lax.axis_index("site")
    mg = lax.axis_index("grp")
    rows_dev, width = noise_ref.shape
    n_loc = sites_ref.shape[0]
    rows = rows_dev * n
    lanes = stat_send.shape[1]
    chunks = site_sem.shape[0]
    crow = n_loc // chunks

    def site_copy(c):
        part = pl.ds(c * crow, crow)
        return pltpu.make_async_copy(sites_ref.at[part, :], sites_v.at[part, :], site_sem.at[c])

    for c in range(chunks):
        site_copy(c).start()
    own = pltpu.make_async_copy(noise_ref, noise_all.at[me], own_sem)
    own.start()

    barrier = pltpu.get_barrier_semaphore()

    def greet_site(k):
        pl.semaphore_signal(barrier, inc=1, device_id={"site": lax.rem(me + k + 1, n)}, device_id_type=MESH)

    def greet_grp(k):
        pl.semaphore_signal(barrier, inc=1, device_id={"grp": lax.rem(mg + k + 1, g)}, device_id_type=MESH)

    steps(n - 1, greet_site)
    steps(g - 1, greet_grp)
    pl.semaphore_wait(barrier, n + g - 2)

    def to_site(src, dst_all, s_sem, r_sem, t):
        return pltpu.make_async_remote_copy(
            src_ref=src, dst_ref=dst_all.at[me], send_sem=s_sem.at[t], recv_sem=r_sem.at[me],
            device_id={"site": t}, device_id_type=MESH)

    def from_site(src, dst_all, s_sem, r_sem, t):
        return pltpu.make_async_remote_copy(
            src_ref=src, dst_ref=dst_all.at[t], send_sem=s_sem.at[t], recv_sem=r_sem.at[t],
            device_id={"site": t}, device_id_type=MESH)

    def other(k):
        return lax.rem(me + k + 1, n)

    steps(n - 1, lambda k: to_site(noise_ref, noise_all, ns_sem, nr_sem, other(k)).start())

    for c in range(chunks):
        site_copy(c).wait()
        acc = None
        for j in range(width // 128):
            x = sites_v[c * crow:(c + 1) * crow, j * 128:(j + 1) * 128].astype(F32)
            acc = x * x if acc is None else acc + x * x
        sq_acc[c * crow:(c + 1) * crow, :] = acc
    half_sq = jnp.sum(sq_acc[...].T, axis=0, keepdims=True) / (2.0 * width)
    own.wait()
    mine = noise_all[me].astype(F32)
    own_sq = jnp.sum(mine * mine, axis=1, keepdims=True) / (2.0 * width)

    steps(n - 1, lambda k: from_site(noise_ref, noise_all, ns_sem, nr_sem, other(k)).wait_recv())
    for d in range(n):
        noise_f[d * rows_dev:(d + 1) * rows_dev, :] = noise_all[d].astype(F32)
    inner = lax.dot_general(noise_f[...].astype(BF16), sites_v[...], (((1,), (1,)), ((), ())),
                            preferred_element_type=F32)
    score = weights_ref[...] + (inner / width - half_sq) / EPS
    top = jnp.max(score, axis=1, keepdims=True)
    shifted = jnp.exp(score - top)
    total = jnp.sum(shifted, axis=1, keepdims=True)
    lse_d = top + jnp.log(total)

    diag = (lax.broadcasted_iota(jnp.int32, (rows, lanes), 0)
            == lax.broadcasted_iota(jnp.int32, (rows, lanes), 1))
    stat_send[...] = jnp.sum(jnp.where(diag, lse_d, 0.0), axis=0, keepdims=True)
    steps(n - 1, lambda k: to_site(stat_send, stat_all, ss_sem, sr_sem, other(k)).start())
    stat_all[me] = stat_send[...]

    probs = shifted.astype(BF16)
    inv = 1.0 / total
    wide = min(1024, width)
    for j in range(width // wide):
        part = jnp.dot(probs, sites_v[:, j * wide:(j + 1) * wide], preferred_element_type=F32)
        t_full[:, j * wide:(j + 1) * wide] = part * inv
    for d in range(n):
        t_send[d] = t_full[d * rows_dev:(d + 1) * rows_dev, :].astype(BF16)

    def t_to(k):
        t = other(k)
        to_site(t_send.at[t], t_all, ts_sem, tr_sem, t).start()

    steps(n - 1, t_to)

    steps(n - 1, lambda k: from_site(stat_send, stat_all, ss_sem, sr_sem, other(k)).wait_recv())
    stats = stat_all[...]
    peak = jnp.max(stats, axis=0)
    lse_row = peak + jnp.log(jnp.sum(jnp.exp(stats - peak[None]), axis=0))
    lse = jnp.sum(jnp.where(diag, lse_row, 0.0), axis=1, keepdims=True)
    mass_part = jnp.sum(jnp.exp(score - lse), axis=0, keepdims=True)
    mass_send[...] = mass_part

    def mass_to(k):
        t = lax.rem(mg + k + 1, g)
        pltpu.make_async_remote_copy(
            src_ref=mass_send, dst_ref=mass_all.at[mg], send_sem=ms_sem.at[t], recv_sem=mr_sem.at[mg],
            device_id={"grp": t}, device_id_type=MESH).start()

    def mass_of(k):
        t = lax.rem(mg + k + 1, g)
        return pltpu.make_async_remote_copy(
            src_ref=mass_send, dst_ref=mass_all.at[t], send_sem=ms_sem.at[t], recv_sem=mr_sem.at[t],
            device_id={"grp": t}, device_id_type=MESH)

    steps(g - 1, mass_to)
    mass_all[mg] = mass_part

    mine_diag = (lax.broadcasted_iota(jnp.int32, (rows_dev, lanes), 0) + me * rows_dev
                 == lax.broadcasted_iota(jnp.int32, (rows_dev, lanes), 1))
    own_lse = jnp.sum(jnp.where(mine_diag, lse_row, 0.0), axis=1, keepdims=True)
    pot = own_sq - EPS * (own_lse - math.log(float(n_loc * n)))
    pot_ref[...] = jnp.broadcast_to(pot, pot_ref.shape)

    t_all[me] = t_send[me]
    steps(n - 1, lambda k: from_site(t_send.at[other(k)], t_all, ts_sem, tr_sem, other(k)).wait_recv())
    acc = None
    for d in range(n):
        share_row = jnp.exp(stat_all[d] - lse_row)
        share = jnp.sum(jnp.where(mine_diag, share_row, 0.0), axis=1, keepdims=True)
        term = share * t_all[d].astype(F32)
        acc = term if acc is None else acc + term
    tgt_ref[...] = acc.astype(BF16)

    steps(g - 1, lambda k: mass_of(k).wait_recv())
    mass = jnp.sum(mass_all[...], axis=0)
    neww_ref[...] = weights_ref[...] + ETA * (1.0 - float(n_loc * n) / float(rows * g) * mass)

    steps(n - 1, lambda k: from_site(noise_ref, noise_all, ns_sem, nr_sem, other(k)).wait_send())
    steps(n - 1, lambda k: from_site(stat_send, stat_all, ss_sem, sr_sem, other(k)).wait_send())
    steps(n - 1, lambda k: from_site(t_send.at[other(k)], t_all, ts_sem, tr_sem, other(k)).wait_send())
    steps(g - 1, lambda k: mass_of(k).wait_send())


def shards(n, g, noise, sites, weights):
    rows_dev, width = noise.shape
    n_loc = sites.shape[0]
    rows = rows_dev * n
    lanes = max(128, rows)
    chunks = 8
    vmem = pl.BlockSpec(memory_space=pltpu.VMEM)
    anym = pl.BlockSpec(memory_space=pl.ANY)
    dma = pltpu.SemaphoreType.DMA
    tgt, pot, neww = pl.pallas_call(
        functools.partial(kernel, n, g),
        out_shape=(
            jax.ShapeDtypeStruct((rows_dev, width), BF16),
            jax.ShapeDtypeStruct((rows_dev, 128), F32),
            jax.ShapeDtypeStruct((1, n_loc), F32),
        ),
        in_specs=[anym, anym, vmem],
        out_specs=(vmem, vmem, vmem),
        scratch_shapes=[
            pltpu.VMEM((n_loc, width), BF16),
            pltpu.VMEM((n, rows_dev, width), BF16),
            pltpu.VMEM((rows, width), F32),
            pltpu.VMEM((n_loc, 128), F32),
            pltpu.VMEM((rows, width), F32),
            pltpu.VMEM((n, rows_dev, width), BF16),
            pltpu.VMEM((n, rows_dev, width), BF16),
            pltpu.VMEM((1, lanes), F32),
            pltpu.VMEM((n, 1, lanes), F32),
            pltpu.VMEM((1, n_loc), F32),
            pltpu.VMEM((g, 1, n_loc), F32),
            dma((chunks,)), dma(()), dma((n,)), dma((n,)), dma((n,)), dma((n,)),
            dma((n,)), dma((n,)), dma((g,)), dma((g,)),
        ],
        compiler_params=pltpu.CompilerParams(
            collective_id=0, has_side_effects=True, vmem_limit_bytes=56 * 1024 * 1024),
        name="dual_step",
    )(noise, sites, weights.reshape(1, n_loc))
    return tgt, pot[:, 0], neww.reshape(n_loc)


def solution(mesh):
    n, g = mesh.shape["site"], mesh.shape["grp"]
    in_specs = (P(("grp", "site"), None), P("site", None), P("site"))
    out_specs = (P(("grp", "site"), None), P(("grp", "site")), P("site"))
    return jax.shard_map(functools.partial(shards, n, g), mesh=mesh, in_specs=in_specs,
                         out_specs=out_specs, check_vma=False)
```

```python
import functools
import math

import jax
import jax.numpy as jnp
from jax import lax
from jax.experimental import pallas as pl
from jax.experimental.pallas import tpu as pltpu
from jax.sharding import PartitionSpec as P

EPS = 0.006
ETA = 0.05
MESH = pl.DeviceIdType.MESH
F32 = jnp.float32
BF16 = jnp.bfloat16


def steps(count, body):
    if count <= 16:
        for k in range(count):
            body(k)
    else:
        lax.fori_loop(0, count, lambda k, c: (body(k), c)[1], 0)


def kernel(n, g, noise_ref, sites_ref, weights_ref, tgt_ref, pot_ref, neww_ref,
           sites_v, weights_v, noise_all, noise_f, sq_acc, t_full, t_send, t_all,
           stat_send, stat_all, mass_send, mass_all,
           site_sem, own_sem, ns_sem, nr_sem, ts_sem, tr_sem, ss_sem, sr_sem, ms_sem, mr_sem):
    me = lax.axis_index("site")
    mg = lax.axis_index("grp")
    rows_dev, width = noise_ref.shape
    n_loc = sites_ref.shape[0]
    rows = rows_dev * n
    lanes = stat_send.shape[1]
    chunks = site_sem.shape[0]
    crow = n_loc // chunks

    def site_copy(c):
        part = pl.ds(c * crow, crow)
        return pltpu.make_async_copy(sites_ref.at[part, :], sites_v.at[part, :], site_sem.at[c])

    barrier = pltpu.get_barrier_semaphore()

    def greet_site(k):
        pl.semaphore_signal(barrier, inc=1, device_id={"site": lax.rem(me + k + 1, n)}, device_id_type=MESH)

    def greet_grp(k):
        pl.semaphore_signal(barrier, inc=1, device_id={"grp": lax.rem(mg + k + 1, g)}, device_id_type=MESH)

    steps(n - 1, greet_site)
    steps(g - 1, greet_grp)
    for c in range(chunks):
        site_copy(c).start()
    own = pltpu.make_async_copy(noise_ref, noise_all.at[me], own_sem.at[0])
    own.start()
    own_w = pltpu.make_async_copy(weights_ref, weights_v, own_sem.at[1])
    own_w.start()
    pl.semaphore_wait(barrier, n + g - 2)

    def to_site(src, dst_all, s_sem, r_sem, t):
        return pltpu.make_async_remote_copy(
            src_ref=src, dst_ref=dst_all.at[me], send_sem=s_sem.at[t], recv_sem=r_sem.at[me],
            device_id={"site": t}, device_id_type=MESH)

    def from_site(src, dst_all, s_sem, r_sem, t):
        return pltpu.make_async_remote_copy(
            src_ref=src, dst_ref=dst_all.at[t], send_sem=s_sem.at[t], recv_sem=r_sem.at[t],
            device_id={"site": t}, device_id_type=MESH)

    def other(k):
        return lax.rem(me + k + 1, n)

    steps(n - 1, lambda k: to_site(noise_ref, noise_all, ns_sem, nr_sem, other(k)).start())

    for c in range(chunks):
        site_copy(c).wait()
        acc = None
        for j in range(width // 128):
            x = sites_v[c * crow:(c + 1) * crow, j * 128:(j + 1) * 128].astype(F32)
            acc = x * x if acc is None else acc + x * x
        sq_acc[c * crow:(c + 1) * crow, :] = acc
    half_sq = jnp.sum(sq_acc[...].T, axis=0, keepdims=True) / (2.0 * width)
    own.wait()
    own_w.wait()
    mine = noise_all[me].astype(F32)
    own_sq = jnp.sum(mine * mine, axis=1, keepdims=True) / (2.0 * width)

    steps(n - 1, lambda k: from_site(noise_ref, noise_all, ns_sem, nr_sem, other(k)).wait_recv())
    for d in range(n):
        noise_f[d * rows_dev:(d + 1) * rows_dev, :] = noise_all[d].astype(F32)
    inner = lax.dot_general(noise_f[...].astype(BF16), sites_v[...], (((1,), (1,)), ((), ())),
                            preferred_element_type=F32)
    score = weights_v[...] + (inner / width - half_sq) / EPS
    top = jnp.max(score, axis=1, keepdims=True)
    shifted = jnp.exp(score - top)
    total = jnp.sum(shifted, axis=1, keepdims=True)
    lse_d = top + jnp.log(total)

    diag = (lax.broadcasted_iota(jnp.int32, (rows, lanes), 0)
            == lax.broadcasted_iota(jnp.int32, (rows, lanes), 1))
    stat_send[...] = jnp.sum(jnp.where(diag, lse_d, 0.0), axis=0, keepdims=True)
    steps(n - 1, lambda k: to_site(stat_send, stat_all, ss_sem, sr_sem, other(k)).start())
    stat_all[me] = stat_send[...]

    probs = shifted.astype(BF16)
    inv = 1.0 / total
    wide = min(1024, width)
    for j in range(width // wide):
        part = jnp.dot(probs, sites_v[:, j * wide:(j + 1) * wide], preferred_element_type=F32)
        t_full[:, j * wide:(j + 1) * wide] = part * inv
    for d in range(n):
        t_send[d] = t_full[d * rows_dev:(d + 1) * rows_dev, :].astype(BF16)

    def t_to(k):
        t = other(k)
        to_site(t_send.at[t], t_all, ts_sem, tr_sem, t).start()

    steps(n - 1, t_to)

    steps(n - 1, lambda k: from_site(stat_send, stat_all, ss_sem, sr_sem, other(k)).wait_recv())
    stats = stat_all[...]
    peak = jnp.max(stats, axis=0)
    lse_row = peak + jnp.log(jnp.sum(jnp.exp(stats - peak[None]), axis=0))
    lse = jnp.sum(jnp.where(diag, lse_row, 0.0), axis=1, keepdims=True)
    mass_part = jnp.sum(jnp.exp(score - lse), axis=0, keepdims=True)
    mass_send[...] = mass_part

    def mass_to(k):
        t = lax.rem(mg + k + 1, g)
        pltpu.make_async_remote_copy(
            src_ref=mass_send, dst_ref=mass_all.at[mg], send_sem=ms_sem.at[t], recv_sem=mr_sem.at[mg],
            device_id={"grp": t}, device_id_type=MESH).start()

    def mass_of(k):
        t = lax.rem(mg + k + 1, g)
        return pltpu.make_async_remote_copy(
            src_ref=mass_send, dst_ref=mass_all.at[t], send_sem=ms_sem.at[t], recv_sem=mr_sem.at[t],
            device_id={"grp": t}, device_id_type=MESH)

    steps(g - 1, mass_to)
    mass_all[mg] = mass_part

    mine_diag = (lax.broadcasted_iota(jnp.int32, (rows_dev, lanes), 0) + me * rows_dev
                 == lax.broadcasted_iota(jnp.int32, (rows_dev, lanes), 1))
    own_lse = jnp.sum(jnp.where(mine_diag, lse_row, 0.0), axis=1, keepdims=True)
    pot = own_sq - EPS * (own_lse - math.log(float(n_loc * n)))
    first = (lax.broadcasted_iota(jnp.int32, (rows_dev, 128), 0)
             == lax.broadcasted_iota(jnp.int32, (rows_dev, 128), 1))
    pot_ref[...] = jnp.sum(jnp.where(first, pot, 0.0), axis=0, keepdims=True)[:, :rows_dev]

    t_all[me] = t_send[me]
    steps(n - 1, lambda k: from_site(t_send.at[other(k)], t_all, ts_sem, tr_sem, other(k)).wait_recv())
    acc = None
    for d in range(n):
        share_row = jnp.exp(stat_all[d] - lse_row)
        share = jnp.sum(jnp.where(mine_diag, share_row, 0.0), axis=1, keepdims=True)
        term = share * t_all[d].astype(F32)
        acc = term if acc is None else acc + term
    tgt_ref[...] = acc.astype(BF16)

    steps(g - 1, lambda k: mass_of(k).wait_recv())
    mass = jnp.sum(mass_all[...], axis=0)
    neww_ref[...] = weights_v[...] + ETA * (1.0 - float(n_loc * n) / float(rows * g) * mass)

    steps(n - 1, lambda k: from_site(noise_ref, noise_all, ns_sem, nr_sem, other(k)).wait_send())
    steps(n - 1, lambda k: from_site(stat_send, stat_all, ss_sem, sr_sem, other(k)).wait_send())
    steps(n - 1, lambda k: from_site(t_send.at[other(k)], t_all, ts_sem, tr_sem, other(k)).wait_send())
    steps(g - 1, lambda k: mass_of(k).wait_send())


def place(tgt, pot, neww, tgt_out, pot_out, neww_out, sems):
    copies = [pltpu.make_async_copy(src, dst, sems.at[i])
              for i, (src, dst) in enumerate(((tgt, tgt_out), (pot, pot_out), (neww, neww_out)))]
    for copy in copies:
        copy.start()
    for copy in copies:
        copy.wait()


def shards(n, g, noise, sites, weights):
    rows_dev, width = noise.shape
    n_loc = sites.shape[0]
    rows = rows_dev * n
    lanes = max(128, rows)
    chunks = 8
    vmem = pl.BlockSpec(memory_space=pltpu.VMEM)
    anym = pl.BlockSpec(memory_space=pl.ANY)
    dma = pltpu.SemaphoreType.DMA
    tgt, pot, neww = pl.pallas_call(
        functools.partial(kernel, n, g),
        out_shape=(
            pltpu.VMEM((rows_dev, width), BF16),
            pltpu.VMEM((1, rows_dev), F32),
            pltpu.VMEM((1, n_loc), F32),
        ),
        in_specs=[anym, anym, anym],
        out_specs=(vmem, vmem, vmem),
        scratch_shapes=[
            pltpu.VMEM((n_loc, width), BF16),
            pltpu.VMEM((1, n_loc), F32),
            pltpu.VMEM((n, rows_dev, width), BF16),
            pltpu.VMEM((rows, width), F32),
            pltpu.VMEM((n_loc, 128), F32),
            pltpu.VMEM((rows, width), F32),
            pltpu.VMEM((n, rows_dev, width), BF16),
            pltpu.VMEM((n, rows_dev, width), BF16),
            pltpu.VMEM((1, lanes), F32),
            pltpu.VMEM((n, 1, lanes), F32),
            pltpu.VMEM((1, n_loc), F32),
            pltpu.VMEM((g, 1, n_loc), F32),
            dma((chunks,)), dma((2,)), dma((n,)), dma((n,)), dma((n,)), dma((n,)),
            dma((n,)), dma((n,)), dma((g,)), dma((g,)),
        ],
        compiler_params=pltpu.CompilerParams(
            collective_id=0, has_side_effects=True, vmem_limit_bytes=56 * 1024 * 1024),
        name="dual_step",
    )(noise, sites, weights.reshape(1, n_loc))
    outs = (tgt, pot.reshape(rows_dev), neww.reshape(n_loc))
    return pl.pallas_call(
        place,
        out_shape=tuple(jax.ShapeDtypeStruct(o.shape, o.dtype) for o in outs),
        in_specs=[anym] * 3,
        out_specs=(anym,) * 3,
        scratch_shapes=[dma((3,))],
        name="place",
    )(*outs)


def solution(mesh):
    n, g = mesh.shape["site"], mesh.shape["grp"]
    in_specs = (P(("grp", "site"), None), P("site", None), P("site"))
    out_specs = (P(("grp", "site"), None), P(("grp", "site")), P("site"))
    return jax.shard_map(functools.partial(shards, n, g), mesh=mesh, in_specs=in_specs,
                         out_specs=out_specs, check_vma=False)
```

```python
import functools
import math

import jax
import jax.numpy as jnp
from jax import lax
from jax.experimental import pallas as pl
from jax.experimental.pallas import tpu as pltpu
from jax.sharding import PartitionSpec as P

EPS = 0.006
ETA = 0.05
MESH = pl.DeviceIdType.MESH
F32 = jnp.float32
BF16 = jnp.bfloat16


def steps(count, body):
    if count <= 16:
        for k in range(count):
            body(k)
    else:
        lax.fori_loop(0, count, lambda k, c: (body(k), c)[1], 0)


def kernel(n, g, noise_ref, sites_ref, weights_ref, tgt_ref, pot_ref, neww_ref,
           sites_v, weights_v, noise_all, noise_f, sq_acc, t_send, t_all,
           stat_send, stat_all, mass_send, mass_all,
           site_sem, own_sem, ns_sem, nr_sem, ts_sem, tr_sem, ss_sem, sr_sem, ms_sem, mr_sem):
    me = lax.axis_index("site")
    mg = lax.axis_index("grp")
    rows_dev, width = noise_ref.shape
    n_loc = sites_ref.shape[0]
    rows = rows_dev * n
    lanes = stat_send.shape[1]
    chunks = site_sem.shape[0]
    crow = n_loc // chunks

    def site_copy(c):
        part = pl.ds(c * crow, crow)
        return pltpu.make_async_copy(sites_ref.at[part, :], sites_v.at[part, :], site_sem.at[c])

    barrier = pltpu.get_barrier_semaphore()

    def greet_site(k):
        pl.semaphore_signal(barrier, inc=1, device_id={"site": lax.rem(me + k + 1, n)}, device_id_type=MESH)

    def greet_grp(k):
        pl.semaphore_signal(barrier, inc=1, device_id={"grp": lax.rem(mg + k + 1, g)}, device_id_type=MESH)

    steps(n - 1, greet_site)
    steps(g - 1, greet_grp)
    for c in range(chunks):
        site_copy(c).start()
    own = pltpu.make_async_copy(noise_ref, noise_all.at[me], own_sem.at[0])
    own.start()
    own_w = pltpu.make_async_copy(weights_ref, weights_v, own_sem.at[1])
    own_w.start()
    pl.semaphore_wait(barrier, n + g - 2)

    def to_site(src, dst, s_sem, r_sem, t):
        pltpu.make_async_remote_copy(
            src_ref=src, dst_ref=dst, send_sem=s_sem, recv_sem=r_sem,
            device_id={"site": t}, device_id_type=MESH).start()

    def drain(blocks, sem):
        pltpu.make_async_copy(blocks, blocks, sem).wait()

    def other(k):
        return lax.rem(me + k + 1, n)

    steps(n - 1, lambda k: to_site(noise_ref, noise_all.at[me], ns_sem, nr_sem, other(k)))

    for c in range(chunks):
        site_copy(c).wait()
        acc = None
        for j in range(width // 128):
            x = sites_v[c * crow:(c + 1) * crow, j * 128:(j + 1) * 128].astype(F32)
            acc = x * x if acc is None else acc + x * x
        sq_acc[c * crow:(c + 1) * crow, :] = acc
    half_sq = jnp.sum(sq_acc[...].T, axis=0, keepdims=True) / (2.0 * width)
    own.wait()
    own_w.wait()
    mine = noise_all[me].astype(F32)
    own_sq = jnp.sum(mine * mine, axis=1, keepdims=True) / (2.0 * width)

    drain(noise_all.at[pl.ds(0, n - 1)], nr_sem)
    for d in range(n):
        noise_f[d * rows_dev:(d + 1) * rows_dev, :] = noise_all[d].astype(F32)
    inner = lax.dot_general(noise_f[...].astype(BF16), sites_v[...], (((1,), (1,)), ((), ())),
                            preferred_element_type=F32)
    score = weights_v[...] + (inner / width - half_sq) / EPS
    top = jnp.max(score, axis=1, keepdims=True)
    shifted = jnp.exp(score - top)
    total = jnp.sum(shifted, axis=1, keepdims=True)
    lse_d = top + jnp.log(total)

    diag = (lax.broadcasted_iota(jnp.int32, (rows, lanes), 0)
            == lax.broadcasted_iota(jnp.int32, (rows, lanes), 1))
    stat_send[...] = jnp.sum(jnp.where(diag, lse_d, 0.0), axis=0, keepdims=True)
    steps(n - 1, lambda k: to_site(stat_send, stat_all.at[me], ss_sem, sr_sem, other(k)))
    stat_all[me] = stat_send[...]

    probs = shifted.astype(BF16)
    inv = 1.0 / total
    parts, wide = t_send.shape[0], t_send.shape[3]
    for c in range(parts):
        part = jnp.dot(probs, sites_v[:, c * wide:(c + 1) * wide], preferred_element_type=F32) * inv
        for d in range(n):
            t_send[c, d] = part[d * rows_dev:(d + 1) * rows_dev, :].astype(BF16)

        def t_to(k):
            t = other(k)
            to_site(t_send.at[c, t], t_all.at[c, me], ts_sem.at[c], tr_sem.at[c], t)

        steps(n - 1, t_to)

    drain(stat_all.at[pl.ds(0, n - 1)], sr_sem)
    stats = stat_all[...]
    peak = jnp.max(stats, axis=0)
    lse_row = peak + jnp.log(jnp.sum(jnp.exp(stats - peak[None]), axis=0))
    lse = jnp.sum(jnp.where(diag, lse_row, 0.0), axis=1, keepdims=True)
    mass_part = jnp.sum(jnp.exp(score - lse), axis=0, keepdims=True)
    mass_send[...] = mass_part

    def mass_to(k):
        pltpu.make_async_remote_copy(
            src_ref=mass_send, dst_ref=mass_all.at[mg], send_sem=ms_sem, recv_sem=mr_sem,
            device_id={"grp": lax.rem(mg + k + 1, g)}, device_id_type=MESH).start()

    steps(g - 1, mass_to)
    mass_all[mg] = mass_part

    mine_diag = (lax.broadcasted_iota(jnp.int32, (rows_dev, lanes), 0) + me * rows_dev
                 == lax.broadcasted_iota(jnp.int32, (rows_dev, lanes), 1))
    own_lse = jnp.sum(jnp.where(mine_diag, lse_row, 0.0), axis=1, keepdims=True)
    pot = own_sq - EPS * (own_lse - math.log(float(n_loc * n)))
    first = (lax.broadcasted_iota(jnp.int32, (rows_dev, 128), 0)
             == lax.broadcasted_iota(jnp.int32, (rows_dev, 128), 1))
    pot_ref[...] = jnp.sum(jnp.where(first, pot, 0.0), axis=0, keepdims=True)[:, :rows_dev]

    shares = []
    for d in range(n):
        share_row = jnp.exp(stat_all[d] - lse_row)
        shares.append(jnp.sum(jnp.where(mine_diag, share_row, 0.0), axis=1, keepdims=True))
    for c in range(parts):
        t_all[c, me] = t_send[c, me]
    for c in range(parts):
        drain(t_all.at[c, pl.ds(0, n - 1)], tr_sem.at[c])
        acc = None
        for d in range(n):
            term = shares[d] * t_all[c, d].astype(F32)
            acc = term if acc is None else acc + term
        tgt_ref[:, c * wide:(c + 1) * wide] = acc.astype(BF16)

    drain(mass_all.at[pl.ds(0, g - 1)], mr_sem)
    mass = jnp.sum(mass_all[...], axis=0)
    neww_ref[...] = weights_v[...] + ETA * (1.0 - float(n_loc * n) / float(rows * g) * mass)

    drain(noise_all.at[pl.ds(0, n - 1)], ns_sem)
    drain(stat_all.at[pl.ds(0, n - 1)], ss_sem)
    for c in range(parts):
        drain(t_all.at[c, pl.ds(0, n - 1)], ts_sem.at[c])
    drain(mass_all.at[pl.ds(0, g - 1)], ms_sem)


def place(tgt, pot, neww, tgt_out, pot_out, neww_out, sems):
    copies = [pltpu.make_async_copy(src, dst, sems.at[i])
              for i, (src, dst) in enumerate(((tgt, tgt_out), (pot, pot_out), (neww, neww_out)))]
    for copy in copies:
        copy.start()
    for copy in copies:
        copy.wait()


def shards(n, g, noise, sites, weights):
    rows_dev, width = noise.shape
    n_loc = sites.shape[0]
    rows = rows_dev * n
    lanes = max(128, rows)
    chunks, parts = 8, 4
    vmem = pl.BlockSpec(memory_space=pltpu.VMEM)
    anym = pl.BlockSpec(memory_space=pl.ANY)
    dma = pltpu.SemaphoreType.DMA
    tgt, pot, neww = pl.pallas_call(
        functools.partial(kernel, n, g),
        out_shape=(
            pltpu.VMEM((rows_dev, width), BF16),
            pltpu.VMEM((1, rows_dev), F32),
            pltpu.VMEM((1, n_loc), F32),
        ),
        in_specs=[anym, anym, anym],
        out_specs=(vmem, vmem, vmem),
        scratch_shapes=[
            pltpu.VMEM((n_loc, width), BF16),
            pltpu.VMEM((1, n_loc), F32),
            pltpu.VMEM((n, rows_dev, width), BF16),
            pltpu.VMEM((rows, width), F32),
            pltpu.VMEM((n_loc, 128), F32),
            pltpu.VMEM((parts, n, rows_dev, width // parts), BF16),
            pltpu.VMEM((parts, n, rows_dev, width // parts), BF16),
            pltpu.VMEM((1, lanes), F32),
            pltpu.VMEM((n, 1, lanes), F32),
            pltpu.VMEM((1, n_loc), F32),
            pltpu.VMEM((g, 1, n_loc), F32),
            dma((chunks,)), dma((2,)), dma(()), dma(()), dma((parts,)), dma((parts,)),
            dma(()), dma(()), dma(()), dma(()),
        ],
        compiler_params=pltpu.CompilerParams(
            collective_id=0, has_side_effects=True, vmem_limit_bytes=56 * 1024 * 1024),
        name="dual_step",
    )(noise, sites, weights.reshape(1, n_loc))
    outs = (tgt, pot.reshape(rows_dev), neww.reshape(n_loc))
    return pl.pallas_call(
        place,
        out_shape=tuple(jax.ShapeDtypeStruct(o.shape, o.dtype) for o in outs),
        in_specs=[vmem] * 3,
        out_specs=(anym,) * 3,
        scratch_shapes=[dma((3,))],
        name="place",
    )(*outs)


def solution(mesh):
    n, g = mesh.shape["site"], mesh.shape["grp"]
    in_specs = (P(("grp", "site"), None), P("site", None), P("site"))
    out_specs = (P(("grp", "site"), None), P(("grp", "site")), P("site"))
    return jax.shard_map(functools.partial(shards, n, g), mesh=mesh, in_specs=in_specs,
                         out_specs=out_specs, check_vma=False)
```

```python
import functools
import math

import jax
import jax.numpy as jnp
from jax import lax
from jax.experimental import pallas as pl
from jax.experimental.pallas import tpu as pltpu
from jax.sharding import PartitionSpec as P

EPS = 0.006
ETA = 0.05
MESH = pl.DeviceIdType.MESH
F32 = jnp.float32
BF16 = jnp.bfloat16


def steps(count, body):
    if count <= 16:
        for k in range(count):
            body(k)
    else:
        lax.fori_loop(0, count, lambda k, c: (body(k), c)[1], 0)


def kernel(n, g, noise_ref, sites_ref, weights_ref, tgt_ref, pot_ref, neww_ref,
           sites_v, weights_v, noise_all, noise_f, sq_acc, t_send, t_all,
           stat_send, stat_all, mass_send, mass_all,
           site_sem, own_sem, ns_sem, nr_sem, ts_sem, tr_sem, ss_sem, sr_sem, ms_sem, mr_sem):
    me = lax.axis_index("site")
    mg = lax.axis_index("grp")
    rows_dev, width = noise_ref.shape
    n_loc = sites_ref.shape[0]
    rows = rows_dev * n
    lanes = stat_send.shape[1]
    chunks = site_sem.shape[0]
    crow = n_loc // chunks
    parts, wide = t_send.shape[0], t_send.shape[3]

    def site_copy(c):
        part = pl.ds(c * crow, crow)
        return pltpu.make_async_copy(sites_ref.at[part, :], sites_v.at[part, :], site_sem.at[c])

    barrier = pltpu.get_barrier_semaphore()

    def greet_site(k):
        pl.semaphore_signal(barrier, inc=1, device_id={"site": lax.rem(me + k + 1, n)}, device_id_type=MESH)

    def greet_grp(k):
        pl.semaphore_signal(barrier, inc=1, device_id={"grp": lax.rem(mg + k + 1, g)}, device_id_type=MESH)

    steps(n - 1, greet_site)
    steps(g - 1, greet_grp)
    for c in range(chunks):
        site_copy(c).start()
    for c in range(parts):
        pltpu.make_async_copy(noise_ref.at[:, pl.ds(c * wide, wide)], noise_all.at[c, me], own_sem.at[0]).start()
    own_w = pltpu.make_async_copy(weights_ref, weights_v, own_sem.at[1])
    own_w.start()
    pl.semaphore_wait(barrier, n + g - 2)

    def to_site(src, dst, s_sem, r_sem, t):
        pltpu.make_async_remote_copy(
            src_ref=src, dst_ref=dst, send_sem=s_sem, recv_sem=r_sem,
            device_id={"site": t}, device_id_type=MESH).start()

    def drain(blocks, sem):
        pltpu.make_async_copy(blocks, blocks, sem).wait()

    def other(k):
        return lax.rem(me + k + 1, n)

    for c in range(parts):
        steps(n - 1, lambda k: to_site(noise_ref.at[:, pl.ds(c * wide, wide)], noise_all.at[c, me],
                                       ns_sem.at[c], nr_sem.at[c], other(k)))

    for c in range(chunks):
        site_copy(c).wait()
        acc = None
        for j in range(width // 128):
            x = sites_v[c * crow:(c + 1) * crow, j * 128:(j + 1) * 128].astype(F32)
            acc = x * x if acc is None else acc + x * x
        sq_acc[c * crow:(c + 1) * crow, :] = acc
    half_sq = jnp.sum(sq_acc[...].T, axis=0, keepdims=True) / (2.0 * width)
    drain(noise_ref, own_sem.at[0])
    own_w.wait()
    own_sq = 0.0
    for c in range(parts):
        mine = noise_all[c, me].astype(F32)
        own_sq = own_sq + jnp.sum(mine * mine, axis=1, keepdims=True)
    own_sq = own_sq / (2.0 * width)

    inner = None
    for c in range(parts):
        drain(noise_all.at[c, pl.ds(0, n - 1)], nr_sem.at[c])
        for d in range(n):
            noise_f[c, d * rows_dev:(d + 1) * rows_dev, :] = noise_all[c, d].astype(F32)
        term = lax.dot_general(noise_f[c].astype(BF16), sites_v[:, c * wide:(c + 1) * wide],
                               (((1,), (1,)), ((), ())), preferred_element_type=F32)
        inner = term if inner is None else inner + term
    score = weights_v[...] + (inner / width - half_sq) / EPS
    top = jnp.max(score, axis=1, keepdims=True)
    shifted = jnp.exp(score - top)
    total = jnp.sum(shifted, axis=1, keepdims=True)
    lse_d = top + jnp.log(total)

    diag = (lax.broadcasted_iota(jnp.int32, (rows, lanes), 0)
            == lax.broadcasted_iota(jnp.int32, (rows, lanes), 1))
    stat_send[...] = jnp.sum(jnp.where(diag, lse_d, 0.0), axis=0, keepdims=True)
    steps(n - 1, lambda k: to_site(stat_send, stat_all.at[me], ss_sem, sr_sem, other(k)))
    stat_all[me] = stat_send[...]

    probs = shifted.astype(BF16)
    inv = 1.0 / total
    for c in range(parts):
        part = jnp.dot(probs, sites_v[:, c * wide:(c + 1) * wide], preferred_element_type=F32) * inv
        for d in range(n):
            t_send[c, d] = part[d * rows_dev:(d + 1) * rows_dev, :].astype(BF16)

        def t_to(k):
            t = other(k)
            to_site(t_send.at[c, t], t_all.at[c, me], ts_sem.at[c], tr_sem.at[c], t)

        steps(n - 1, t_to)

    drain(stat_all.at[pl.ds(0, n - 1)], sr_sem)
    stats = stat_all[...]
    peak = jnp.max(stats, axis=0)
    lse_row = peak + jnp.log(jnp.sum(jnp.exp(stats - peak[None]), axis=0))
    lse = jnp.sum(jnp.where(diag, lse_row, 0.0), axis=1, keepdims=True)
    mass_part = jnp.sum(jnp.exp(score - lse), axis=0, keepdims=True)
    mass_send[...] = mass_part

    def mass_to(k):
        pltpu.make_async_remote_copy(
            src_ref=mass_send, dst_ref=mass_all.at[mg], send_sem=ms_sem, recv_sem=mr_sem,
            device_id={"grp": lax.rem(mg + k + 1, g)}, device_id_type=MESH).start()

    steps(g - 1, mass_to)
    mass_all[mg] = mass_part

    mine_diag = (lax.broadcasted_iota(jnp.int32, (rows_dev, lanes), 0) + me * rows_dev
                 == lax.broadcasted_iota(jnp.int32, (rows_dev, lanes), 1))
    own_lse = jnp.sum(jnp.where(mine_diag, lse_row, 0.0), axis=1, keepdims=True)
    pot = own_sq - EPS * (own_lse - math.log(float(n_loc * n)))
    first = (lax.broadcasted_iota(jnp.int32, (rows_dev, 128), 0)
             == lax.broadcasted_iota(jnp.int32, (rows_dev, 128), 1))
    pot_ref[...] = jnp.sum(jnp.where(first, pot, 0.0), axis=0, keepdims=True)[:, :rows_dev]

    shares = []
    for d in range(n):
        share_row = jnp.exp(stat_all[d] - lse_row)
        shares.append(jnp.sum(jnp.where(mine_diag, share_row, 0.0), axis=1, keepdims=True))
    for c in range(parts):
        t_all[c, me] = t_send[c, me]
    for c in range(parts):
        drain(t_all.at[c, pl.ds(0, n - 1)], tr_sem.at[c])
        acc = None
        for d in range(n):
            term = shares[d] * t_all[c, d].astype(F32)
            acc = term if acc is None else acc + term
        tgt_ref[:, c * wide:(c + 1) * wide] = acc.astype(BF16)

    drain(mass_all.at[pl.ds(0, g - 1)], mr_sem)
    mass = jnp.sum(mass_all[...], axis=0)
    neww_ref[...] = weights_v[...] + ETA * (1.0 - float(n_loc * n) / float(rows * g) * mass)

    drain(stat_all.at[pl.ds(0, n - 1)], ss_sem)
    for c in range(parts):
        drain(noise_all.at[c, pl.ds(0, n - 1)], ns_sem.at[c])
        drain(t_all.at[c, pl.ds(0, n - 1)], ts_sem.at[c])
    drain(mass_all.at[pl.ds(0, g - 1)], ms_sem)


def place(tgt, pot, neww, tgt_out, pot_out, neww_out, sems):
    copies = [pltpu.make_async_copy(src, dst, sems.at[i])
              for i, (src, dst) in enumerate(((tgt, tgt_out), (pot, pot_out), (neww, neww_out)))]
    for copy in copies:
        copy.start()
    for copy in copies:
        copy.wait()


def shards(n, g, noise, sites, weights):
    rows_dev, width = noise.shape
    n_loc = sites.shape[0]
    rows = rows_dev * n
    lanes = max(128, rows)
    chunks, parts = 8, 4
    vmem = pl.BlockSpec(memory_space=pltpu.VMEM)
    anym = pl.BlockSpec(memory_space=pl.ANY)
    dma = pltpu.SemaphoreType.DMA
    tgt, pot, neww = pl.pallas_call(
        functools.partial(kernel, n, g),
        out_shape=(
            pltpu.VMEM((rows_dev, width), BF16),
            pltpu.VMEM((1, rows_dev), F32),
            pltpu.VMEM((1, n_loc), F32),
        ),
        in_specs=[anym, anym, anym],
        out_specs=(vmem, vmem, vmem),
        scratch_shapes=[
            pltpu.VMEM((n_loc, width), BF16),
            pltpu.VMEM((1, n_loc), F32),
            pltpu.VMEM((parts, n, rows_dev, width // parts), BF16),
            pltpu.VMEM((parts, rows, width // parts), F32),
            pltpu.VMEM((n_loc, 128), F32),
            pltpu.VMEM((parts, n, rows_dev, width // parts), BF16),
            pltpu.VMEM((parts, n, rows_dev, width // parts), BF16),
            pltpu.VMEM((1, lanes), F32),
            pltpu.VMEM((n, 1, lanes), F32),
            pltpu.VMEM((1, n_loc), F32),
            pltpu.VMEM((g, 1, n_loc), F32),
            dma((chunks,)), dma((2,)), dma((parts,)), dma((parts,)), dma((parts,)), dma((parts,)),
            dma(()), dma(()), dma(()), dma(()),
        ],
        compiler_params=pltpu.CompilerParams(
            collective_id=0, has_side_effects=True, vmem_limit_bytes=56 * 1024 * 1024),
        name="dual_step",
    )(noise, sites, weights.reshape(1, n_loc))
    outs = (tgt, pot.reshape(rows_dev), neww.reshape(n_loc))
    return pl.pallas_call(
        place,
        out_shape=tuple(jax.ShapeDtypeStruct(o.shape, o.dtype) for o in outs),
        in_specs=[vmem] * 3,
        out_specs=(anym,) * 3,
        scratch_shapes=[dma((3,))],
        compiler_params=pltpu.CompilerParams(vmem_limit_bytes=1024 * 1024),
        name="place",
    )(*outs)


def solution(mesh):
    n, g = mesh.shape["site"], mesh.shape["grp"]
    in_specs = (P(("grp", "site"), None), P("site", None), P("site"))
    out_specs = (P(("grp", "site"), None), P(("grp", "site")), P("site"))
    return jax.shard_map(functools.partial(shards, n, g), mesh=mesh, in_specs=in_specs,
                         out_specs=out_specs, check_vma=False)
```

```python
import functools
import math

import jax
import jax.numpy as jnp
from jax import lax
from jax.experimental import pallas as pl
from jax.experimental.pallas import tpu as pltpu
from jax.sharding import PartitionSpec as P

EPS = 0.006
ETA = 0.05
MESH = pl.DeviceIdType.MESH
F32 = jnp.float32
BF16 = jnp.bfloat16


def steps(count, body):
    if count <= 16:
        for k in range(count):
            body(k)
    else:
        lax.fori_loop(0, count, lambda k, c: (body(k), c)[1], 0)


def kernel(n, g, noise_ref, sites_ref, weights_ref, tgt_ref, pot_ref, neww_ref,
           sites_v, weights_v, noise_all, noise_f, sq_acc, t_send, t_all,
           stat_send, stat_all, mass_send, mass_all,
           site_sem, own_sem, ns_sem, nr_sem, ts_sem, tr_sem, ss_sem, sr_sem, ms_sem, mr_sem):
    me = lax.axis_index("site")
    mg = lax.axis_index("grp")
    rows_dev, width = noise_ref.shape
    n_loc = sites_ref.shape[0]
    rows = rows_dev * n
    lanes = stat_send.shape[1]
    chunks = site_sem.shape[0]
    crow = n_loc // chunks
    parts, wide = t_send.shape[0], t_send.shape[3]

    def site_copy(c):
        part = pl.ds(c * crow, crow)
        return pltpu.make_async_copy(sites_ref.at[part, :], sites_v.at[part, :], site_sem.at[c])

    barrier = pltpu.get_barrier_semaphore()

    def greet_site(k):
        pl.semaphore_signal(barrier, inc=1, device_id={"site": lax.rem(me + k + 1, n)}, device_id_type=MESH)

    def greet_grp(k):
        pl.semaphore_signal(barrier, inc=1, device_id={"grp": lax.rem(mg + k + 1, g)}, device_id_type=MESH)

    steps(n - 1, greet_site)
    steps(g - 1, greet_grp)
    for c in range(chunks):
        site_copy(c).start()
    for c in range(parts):
        pltpu.make_async_copy(noise_ref.at[:, pl.ds(c * wide, wide)], noise_all.at[c, me], own_sem.at[0]).start()
    own_w = pltpu.make_async_copy(weights_ref, weights_v, own_sem.at[1])
    own_w.start()
    pl.semaphore_wait(barrier, n + g - 2)

    def to_site(src, dst, s_sem, r_sem, t):
        pltpu.make_async_remote_copy(
            src_ref=src, dst_ref=dst, send_sem=s_sem, recv_sem=r_sem,
            device_id={"site": t}, device_id_type=MESH).start()

    def drain(blocks, sem):
        pltpu.make_async_copy(blocks, blocks, sem).wait()

    def other(k):
        return lax.rem(me + k + 1, n)

    for c in range(parts):
        steps(n - 1, lambda k: to_site(noise_ref.at[:, pl.ds(c * wide, wide)], noise_all.at[c, me],
                                       ns_sem.at[c], nr_sem.at[c], other(k)))

    for c in range(chunks):
        site_copy(c).wait()
        acc = None
        for j in range(width // 128):
            x = sites_v[c * crow:(c + 1) * crow, j * 128:(j + 1) * 128].astype(F32)
            acc = x * x if acc is None else acc + x * x
        sq_acc[c * crow:(c + 1) * crow, :] = acc
    half_sq = jnp.sum(sq_acc[...].T, axis=0, keepdims=True) / (2.0 * width)
    drain(noise_ref, own_sem.at[0])
    own_w.wait()
    own_sq = 0.0
    for c in range(parts):
        mine = noise_all[c, me].astype(F32)
        own_sq = own_sq + jnp.sum(mine * mine, axis=1, keepdims=True)
    own_sq = own_sq / (2.0 * width)

    inner = None
    for c in range(parts):
        drain(noise_all.at[c, pl.ds(0, n - 1)], nr_sem.at[c])
        for d in range(n):
            noise_f[c, d * rows_dev:(d + 1) * rows_dev, :] = noise_all[c, d].astype(F32)
        term = lax.dot_general(sites_v[:, c * wide:(c + 1) * wide], noise_f[c].astype(BF16),
                               (((1,), (1,)), ((), ())), preferred_element_type=F32)
        inner = term if inner is None else inner + term
    inner = inner.T
    score = weights_v[...] + (inner / width - half_sq) / EPS
    top = jnp.max(score, axis=1, keepdims=True)
    shifted = jnp.exp(score - top)
    total = jnp.sum(shifted, axis=1, keepdims=True)
    lse_d = top + jnp.log(total)

    diag = (lax.broadcasted_iota(jnp.int32, (rows, lanes), 0)
            == lax.broadcasted_iota(jnp.int32, (rows, lanes), 1))
    stat_send[...] = jnp.sum(jnp.where(diag, lse_d, 0.0), axis=0, keepdims=True)
    steps(n - 1, lambda k: to_site(stat_send, stat_all.at[me], ss_sem, sr_sem, other(k)))
    stat_all[me] = stat_send[...]

    probs = shifted.astype(BF16)
    inv = 1.0 / total
    for c in range(parts):
        part = jnp.dot(probs, sites_v[:, c * wide:(c + 1) * wide], preferred_element_type=F32) * inv
        for d in range(n):
            t_send[c, d] = part[d * rows_dev:(d + 1) * rows_dev, :].astype(BF16)

        def t_to(k):
            t = other(k)
            to_site(t_send.at[c, t], t_all.at[c, me], ts_sem.at[c], tr_sem.at[c], t)

        steps(n - 1, t_to)

    drain(stat_all.at[pl.ds(0, n - 1)], sr_sem)
    stats = stat_all[...]
    peak = jnp.max(stats, axis=0)
    lse_row = peak + jnp.log(jnp.sum(jnp.exp(stats - peak[None]), axis=0))
    lse = jnp.sum(jnp.where(diag, lse_row, 0.0), axis=1, keepdims=True)
    mass_part = jnp.sum(jnp.exp(score - lse), axis=0, keepdims=True)
    mass_send[...] = mass_part

    def mass_to(k):
        pltpu.make_async_remote_copy(
            src_ref=mass_send, dst_ref=mass_all.at[mg], send_sem=ms_sem, recv_sem=mr_sem,
            device_id={"grp": lax.rem(mg + k + 1, g)}, device_id_type=MESH).start()

    steps(g - 1, mass_to)
    mass_all[mg] = mass_part

    mine_diag = (lax.broadcasted_iota(jnp.int32, (rows_dev, lanes), 0) + me * rows_dev
                 == lax.broadcasted_iota(jnp.int32, (rows_dev, lanes), 1))
    own_lse = jnp.sum(jnp.where(mine_diag, lse_row, 0.0), axis=1, keepdims=True)
    pot = own_sq - EPS * (own_lse - math.log(float(n_loc * n)))
    first = (lax.broadcasted_iota(jnp.int32, (rows_dev, 128), 0)
             == lax.broadcasted_iota(jnp.int32, (rows_dev, 128), 1))
    pot_ref[...] = jnp.sum(jnp.where(first, pot, 0.0), axis=0, keepdims=True)[:, :rows_dev]

    shares = []
    for d in range(n):
        share_row = jnp.exp(stat_all[d] - lse_row)
        shares.append(jnp.sum(jnp.where(mine_diag, share_row, 0.0), axis=1, keepdims=True))
    for c in range(parts):
        t_all[c, me] = t_send[c, me]
    for c in range(parts):
        drain(t_all.at[c, pl.ds(0, n - 1)], tr_sem.at[c])
        acc = None
        for d in range(n):
            term = shares[d] * t_all[c, d].astype(F32)
            acc = term if acc is None else acc + term
        tgt_ref[:, c * wide:(c + 1) * wide] = acc.astype(BF16)

    drain(mass_all.at[pl.ds(0, g - 1)], mr_sem)
    mass = jnp.sum(mass_all[...], axis=0)
    neww_ref[...] = weights_v[...] + ETA * (1.0 - float(n_loc * n) / float(rows * g) * mass)

    drain(stat_all.at[pl.ds(0, n - 1)], ss_sem)
    for c in range(parts):
        drain(noise_all.at[c, pl.ds(0, n - 1)], ns_sem.at[c])
        drain(t_all.at[c, pl.ds(0, n - 1)], ts_sem.at[c])
    drain(mass_all.at[pl.ds(0, g - 1)], ms_sem)


def place(tgt, pot, neww, tgt_out, pot_out, neww_out, sems):
    copies = [pltpu.make_async_copy(src, dst, sems.at[i])
              for i, (src, dst) in enumerate(((tgt, tgt_out), (pot, pot_out), (neww, neww_out)))]
    for copy in copies:
        copy.start()
    for copy in copies:
        copy.wait()


def shards(n, g, noise, sites, weights):
    rows_dev, width = noise.shape
    n_loc = sites.shape[0]
    rows = rows_dev * n
    lanes = max(128, rows)
    chunks, parts = 8, 4
    vmem = pl.BlockSpec(memory_space=pltpu.VMEM)
    anym = pl.BlockSpec(memory_space=pl.ANY)
    dma = pltpu.SemaphoreType.DMA
    tgt, pot, neww = pl.pallas_call(
        functools.partial(kernel, n, g),
        out_shape=(
            pltpu.VMEM((rows_dev, width), BF16),
            pltpu.VMEM((1, rows_dev), F32),
            pltpu.VMEM((1, n_loc), F32),
        ),
        in_specs=[anym, anym, anym],
        out_specs=(vmem, vmem, vmem),
        scratch_shapes=[
            pltpu.VMEM((n_loc, width), BF16),
            pltpu.VMEM((1, n_loc), F32),
            pltpu.VMEM((parts, n, rows_dev, width // parts), BF16),
            pltpu.VMEM((parts, rows, width // parts), F32),
            pltpu.VMEM((n_loc, 128), F32),
            pltpu.VMEM((parts, n, rows_dev, width // parts), BF16),
            pltpu.VMEM((parts, n, rows_dev, width // parts), BF16),
            pltpu.VMEM((1, lanes), F32),
            pltpu.VMEM((n, 1, lanes), F32),
            pltpu.VMEM((1, n_loc), F32),
            pltpu.VMEM((g, 1, n_loc), F32),
            dma((chunks,)), dma((2,)), dma((parts,)), dma((parts,)), dma((parts,)), dma((parts,)),
            dma(()), dma(()), dma(()), dma(()),
        ],
        compiler_params=pltpu.CompilerParams(
            collective_id=0, has_side_effects=True, vmem_limit_bytes=56 * 1024 * 1024),
        name="dual_step",
    )(noise, sites, weights.reshape(1, n_loc))
    outs = (tgt, pot.reshape(rows_dev), neww.reshape(n_loc))
    return pl.pallas_call(
        place,
        out_shape=tuple(jax.ShapeDtypeStruct(o.shape, o.dtype) for o in outs),
        in_specs=[vmem] * 3,
        out_specs=(anym,) * 3,
        scratch_shapes=[dma((3,))],
        compiler_params=pltpu.CompilerParams(vmem_limit_bytes=1024 * 1024),
        name="place",
    )(*outs)


def solution(mesh):
    n, g = mesh.shape["site"], mesh.shape["grp"]
    in_specs = (P(("grp", "site"), None), P("site", None), P("site"))
    out_specs = (P(("grp", "site"), None), P(("grp", "site")), P("site"))
    return jax.shard_map(functools.partial(shards, n, g), mesh=mesh, in_specs=in_specs,
                         out_specs=out_specs, check_vma=False)
```

```python
import functools
import math

import jax
import jax.numpy as jnp
from jax import lax
from jax.experimental import pallas as pl
from jax.experimental.pallas import tpu as pltpu
from jax.sharding import PartitionSpec as P

EPS = 0.006
ETA = 0.05
MESH = pl.DeviceIdType.MESH
F32 = jnp.float32
BF16 = jnp.bfloat16


def steps(count, body):
    if count <= 16:
        for k in range(count):
            body(k)
    else:
        lax.fori_loop(0, count, lambda k, c: (body(k), c)[1], 0)


def kernel(n, g, noise_ref, sites_ref, weights_ref, tgt_ref, pot_ref, neww_ref,
           sites_v, weights_v, noise_all, noise_f, sq_acc, t_send, t_all,
           stat_send, stat_all, mass_send, mass_all,
           site_sem, own_sem, ns_sem, nr_sem, ts_sem, tr_sem, ss_sem, sr_sem, ms_sem, mr_sem):
    me = lax.axis_index("site")
    mg = lax.axis_index("grp")
    rows_dev, width = noise_ref.shape
    n_loc = sites_ref.shape[0]
    rows = rows_dev * n
    lanes = stat_send.shape[1]
    chunks = site_sem.shape[0]
    crow = n_loc // chunks
    parts, wide = t_send.shape[0], t_send.shape[3]

    def site_copy(c):
        part = pl.ds(c * crow, crow)
        return pltpu.make_async_copy(sites_ref.at[part, :], sites_v.at[part, :], site_sem.at[c])

    barrier = pltpu.get_barrier_semaphore()

    def greet_site(k):
        pl.semaphore_signal(barrier, inc=1, device_id={"site": lax.rem(me + k + 1, n)}, device_id_type=MESH)

    def greet_grp(k):
        pl.semaphore_signal(barrier, inc=1, device_id={"grp": lax.rem(mg + k + 1, g)}, device_id_type=MESH)

    steps(n - 1, greet_site)
    steps(g - 1, greet_grp)
    for c in range(chunks):
        site_copy(c).start()
    for c in range(parts):
        pltpu.make_async_copy(noise_ref.at[:, pl.ds(c * wide, wide)], noise_all.at[c, me], own_sem.at[0]).start()
    own_w = pltpu.make_async_copy(weights_ref, weights_v, own_sem.at[1])
    own_w.start()
    pl.semaphore_wait(barrier, n + g - 2)

    def to_site(src, dst, s_sem, r_sem, t):
        pltpu.make_async_remote_copy(
            src_ref=src, dst_ref=dst, send_sem=s_sem, recv_sem=r_sem,
            device_id={"site": t}, device_id_type=MESH).start()

    def drain(blocks, sem):
        pltpu.make_async_copy(blocks, blocks, sem).wait()

    def other(k):
        return lax.rem(me + k + 1, n)

    def columns(c):
        return pl.ds(pl.multiple_of(c * wide, wide), wide)

    def noise_to(c, carry):
        steps(n - 1, lambda k: to_site(noise_ref.at[:, columns(c)], noise_all.at[c, me],
                                       ns_sem.at[c], nr_sem.at[c], other(k)))
        return carry

    lax.fori_loop(0, parts, noise_to, 0)

    def squares(c, carry):
        site_copy(c).wait()
        part = pl.ds(pl.multiple_of(c * crow, crow), crow)
        acc = None
        for j in range(width // 128):
            x = sites_v[part, j * 128:(j + 1) * 128].astype(F32)
            acc = x * x if acc is None else acc + x * x
        sq_acc[part, :] = acc
        return carry

    lax.fori_loop(0, chunks, squares, 0)
    half_sq = jnp.sum(sq_acc[...].T, axis=0, keepdims=True) / (2.0 * width)
    drain(noise_ref, own_sem.at[0])
    own_w.wait()
    own_sq = 0.0
    for c in range(parts):
        mine = noise_all[c, me].astype(F32)
        own_sq = own_sq + jnp.sum(mine * mine, axis=1, keepdims=True)
    own_sq = own_sq / (2.0 * width)

    def inner_part(c, inner):
        drain(noise_all.at[c, pl.ds(0, n - 1)], nr_sem.at[c])
        for d in range(n):
            noise_f[d * rows_dev:(d + 1) * rows_dev, :] = noise_all[c, d].astype(F32)
        return inner + lax.dot_general(noise_f[...].astype(BF16), sites_v[:, columns(c)],
                                       (((1,), (1,)), ((), ())), preferred_element_type=F32)

    inner = lax.fori_loop(0, parts, inner_part, jnp.zeros((rows, n_loc), F32))
    score = weights_v[...] + (inner / width - half_sq) / EPS
    top = jnp.max(score, axis=1, keepdims=True)
    shifted = jnp.exp(score - top)
    total = jnp.sum(shifted, axis=1, keepdims=True)
    lse_d = top + jnp.log(total)

    diag = (lax.broadcasted_iota(jnp.int32, (rows, lanes), 0)
            == lax.broadcasted_iota(jnp.int32, (rows, lanes), 1))
    stat_send[...] = jnp.sum(jnp.where(diag, lse_d, 0.0), axis=0, keepdims=True)
    steps(n - 1, lambda k: to_site(stat_send, stat_all.at[me], ss_sem, sr_sem, other(k)))
    stat_all[me] = stat_send[...]

    probs = shifted.astype(BF16)
    inv = 1.0 / total
    def targets(c, carry):
        part = jnp.dot(probs, sites_v[:, columns(c)], preferred_element_type=F32) * inv
        for d in range(n):
            t_send[c, d] = part[d * rows_dev:(d + 1) * rows_dev, :].astype(BF16)

        def t_to(k):
            t = other(k)
            to_site(t_send.at[c, t], t_all.at[c, me], ts_sem.at[c], tr_sem.at[c], t)

        steps(n - 1, t_to)
        return carry

    lax.fori_loop(0, parts, targets, 0)

    drain(stat_all.at[pl.ds(0, n - 1)], sr_sem)
    stats = stat_all[...]
    peak = jnp.max(stats, axis=0)
    lse_row = peak + jnp.log(jnp.sum(jnp.exp(stats - peak[None]), axis=0))
    lse = jnp.sum(jnp.where(diag, lse_row, 0.0), axis=1, keepdims=True)
    mass_part = jnp.sum(jnp.exp(score - lse), axis=0, keepdims=True)
    mass_send[...] = mass_part

    def mass_to(k):
        pltpu.make_async_remote_copy(
            src_ref=mass_send, dst_ref=mass_all.at[mg], send_sem=ms_sem, recv_sem=mr_sem,
            device_id={"grp": lax.rem(mg + k + 1, g)}, device_id_type=MESH).start()

    steps(g - 1, mass_to)
    mass_all[mg] = mass_part

    mine_diag = (lax.broadcasted_iota(jnp.int32, (rows_dev, lanes), 0) + me * rows_dev
                 == lax.broadcasted_iota(jnp.int32, (rows_dev, lanes), 1))
    own_lse = jnp.sum(jnp.where(mine_diag, lse_row, 0.0), axis=1, keepdims=True)
    pot = own_sq - EPS * (own_lse - math.log(float(n_loc * n)))
    first = (lax.broadcasted_iota(jnp.int32, (rows_dev, 128), 0)
             == lax.broadcasted_iota(jnp.int32, (rows_dev, 128), 1))
    pot_ref[...] = jnp.sum(jnp.where(first, pot, 0.0), axis=0, keepdims=True)[:, :rows_dev]

    shares = []
    for d in range(n):
        share_row = jnp.exp(stat_all[d] - lse_row)
        shares.append(jnp.sum(jnp.where(mine_diag, share_row, 0.0), axis=1, keepdims=True))
    for c in range(parts):
        t_all[c, me] = t_send[c, me]
    def combine(c, carry):
        drain(t_all.at[c, pl.ds(0, n - 1)], tr_sem.at[c])
        acc = None
        for d in range(n):
            term = shares[d] * t_all[c, d].astype(F32)
            acc = term if acc is None else acc + term
        tgt_ref[:, columns(c)] = acc.astype(BF16)
        return carry

    lax.fori_loop(0, parts, combine, 0)

    drain(mass_all.at[pl.ds(0, g - 1)], mr_sem)
    mass = jnp.sum(mass_all[...], axis=0)
    neww_ref[...] = weights_v[...] + ETA * (1.0 - float(n_loc * n) / float(rows * g) * mass)

    drain(stat_all.at[pl.ds(0, n - 1)], ss_sem)
    for c in range(parts):
        drain(noise_all.at[c, pl.ds(0, n - 1)], ns_sem.at[c])
        drain(t_all.at[c, pl.ds(0, n - 1)], ts_sem.at[c])
    drain(mass_all.at[pl.ds(0, g - 1)], ms_sem)


def place(tgt, pot, neww, tgt_out, pot_out, neww_out, sems):
    copies = [pltpu.make_async_copy(src, dst, sems.at[i])
              for i, (src, dst) in enumerate(((tgt, tgt_out), (pot, pot_out), (neww, neww_out)))]
    for copy in copies:
        copy.start()
    for copy in copies:
        copy.wait()


def shards(n, g, noise, sites, weights):
    rows_dev, width = noise.shape
    n_loc = sites.shape[0]
    rows = rows_dev * n
    lanes = max(128, rows)
    chunks, parts = 8, 4
    vmem = pl.BlockSpec(memory_space=pltpu.VMEM)
    anym = pl.BlockSpec(memory_space=pl.ANY)
    dma = pltpu.SemaphoreType.DMA
    tgt, pot, neww = pl.pallas_call(
        functools.partial(kernel, n, g),
        out_shape=(
            pltpu.VMEM((rows_dev, width), BF16),
            pltpu.VMEM((1, rows_dev), F32),
            pltpu.VMEM((1, n_loc), F32),
        ),
        in_specs=[anym, anym, anym],
        out_specs=(vmem, vmem, vmem),
        scratch_shapes=[
            pltpu.VMEM((n_loc, width), BF16),
            pltpu.VMEM((1, n_loc), F32),
            pltpu.VMEM((parts, n, rows_dev, width // parts), BF16),
            pltpu.VMEM((rows, width // parts), F32),
            pltpu.VMEM((n_loc, 128), F32),
            pltpu.VMEM((parts, n, rows_dev, width // parts), BF16),
            pltpu.VMEM((parts, n, rows_dev, width // parts), BF16),
            pltpu.VMEM((1, lanes), F32),
            pltpu.VMEM((n, 1, lanes), F32),
            pltpu.VMEM((1, n_loc), F32),
            pltpu.VMEM((g, 1, n_loc), F32),
            dma((chunks,)), dma((2,)), dma((parts,)), dma((parts,)), dma((parts,)), dma((parts,)),
            dma(()), dma(()), dma(()), dma(()),
        ],
        compiler_params=pltpu.CompilerParams(
            collective_id=0, has_side_effects=True, vmem_limit_bytes=56 * 1024 * 1024),
        name="dual_step",
    )(noise, sites, weights.reshape(1, n_loc))
    outs = (tgt, pot.reshape(rows_dev), neww.reshape(n_loc))
    return pl.pallas_call(
        place,
        out_shape=tuple(jax.ShapeDtypeStruct(o.shape, o.dtype) for o in outs),
        in_specs=[vmem] * 3,
        out_specs=(anym,) * 3,
        scratch_shapes=[dma((3,))],
        compiler_params=pltpu.CompilerParams(vmem_limit_bytes=1024 * 1024),
        name="place",
    )(*outs)


def solution(mesh):
    n, g = mesh.shape["site"], mesh.shape["grp"]
    in_specs = (P(("grp", "site"), None), P("site", None), P("site"))
    out_specs = (P(("grp", "site"), None), P(("grp", "site")), P("site"))
    return jax.shard_map(functools.partial(shards, n, g), mesh=mesh, in_specs=in_specs,
                         out_specs=out_specs, check_vma=False)
```

```python
import functools
import math

import jax
import jax.numpy as jnp
from jax import lax
from jax.experimental import pallas as pl
from jax.experimental.pallas import tpu as pltpu
from jax.sharding import PartitionSpec as P

EPS = 0.006
ETA = 0.05
MESH = pl.DeviceIdType.MESH
F32 = jnp.float32
BF16 = jnp.bfloat16


def steps(count, body):
    if count <= 16:
        for k in range(count):
            body(k)
    else:
        lax.fori_loop(0, count, lambda k, c: (body(k), c)[1], 0)


def kernel(n, g, noise_ref, sites_ref, weights_ref, tgt_ref, pot_ref, neww_ref,
           sites_v, weights_v, noise_all, noise_f, sq_acc, t_send, t_all,
           stat_send, stat_all, mass_send, mass_all,
           site_sem, own_sem, ns_sem, nr_sem, ts_sem, tr_sem, ss_sem, sr_sem, ms_sem, mr_sem):
    me = lax.axis_index("site")
    mg = lax.axis_index("grp")
    rows_dev, width = noise_ref.shape
    n_loc = sites_ref.shape[0]
    rows = rows_dev * n
    lanes = stat_send.shape[1]
    chunks = site_sem.shape[0]
    crow = n_loc // chunks
    parts, wide = t_send.shape[0], t_send.shape[3]
    n_parts, n_wide = noise_all.shape[0], noise_all.shape[3]

    def site_copy(c):
        part = pl.ds(c * crow, crow)
        return pltpu.make_async_copy(sites_ref.at[part, :], sites_v.at[part, :], site_sem.at[c])

    barrier = pltpu.get_barrier_semaphore()

    def greet_site(k):
        pl.semaphore_signal(barrier, inc=1, device_id={"site": lax.rem(me + k + 1, n)}, device_id_type=MESH)

    def greet_grp(k):
        pl.semaphore_signal(barrier, inc=1, device_id={"grp": lax.rem(mg + k + 1, g)}, device_id_type=MESH)

    steps(n - 1, greet_site)
    steps(g - 1, greet_grp)
    for c in range(chunks):
        site_copy(c).start()
    pl.semaphore_wait(barrier, n + g - 2)

    def to_site(src, dst, s_sem, r_sem, t):
        pltpu.make_async_remote_copy(
            src_ref=src, dst_ref=dst, send_sem=s_sem, recv_sem=r_sem,
            device_id={"site": t}, device_id_type=MESH).start()

    def drain(blocks, sem):
        pltpu.make_async_copy(blocks, blocks, sem).wait()

    def other(k):
        return lax.rem(me + k + 1, n)

    for c in range(n_parts):
        steps(n - 1, lambda k: to_site(noise_ref.at[:, pl.ds(c * n_wide, n_wide)], noise_all.at[c, me],
                                       ns_sem.at[c], nr_sem.at[c], other(k)))
    for c in range(n_parts):
        pltpu.make_async_copy(noise_ref.at[:, pl.ds(c * n_wide, n_wide)], noise_all.at[c, me], own_sem.at[0]).start()
    own_w = pltpu.make_async_copy(weights_ref, weights_v, own_sem.at[1])
    own_w.start()

    for c in range(chunks):
        site_copy(c).wait()
        acc = None
        for j in range(width // 128):
            x = sites_v[c * crow:(c + 1) * crow, j * 128:(j + 1) * 128].astype(F32)
            acc = x * x if acc is None else acc + x * x
        sq_acc[c * crow:(c + 1) * crow, :] = acc
    half_sq = jnp.sum(sq_acc[...].T, axis=0, keepdims=True) / (2.0 * width)
    drain(noise_ref, own_sem.at[0])
    own_w.wait()
    own_sq = 0.0
    for c in range(n_parts):
        mine = noise_all[c, me].astype(F32)
        own_sq = own_sq + jnp.sum(mine * mine, axis=1, keepdims=True)
    own_sq = own_sq / (2.0 * width)

    inner = None
    for c in range(n_parts):
        drain(noise_all.at[c, pl.ds(0, n - 1)], nr_sem.at[c])
        for d in range(n):
            noise_f[c, d * rows_dev:(d + 1) * rows_dev, :] = noise_all[c, d].astype(F32)
        term = lax.dot_general(noise_f[c].astype(BF16), sites_v[:, c * n_wide:(c + 1) * n_wide],
                               (((1,), (1,)), ((), ())), preferred_element_type=F32)
        inner = term if inner is None else inner + term
    score = weights_v[...] + (inner / width - half_sq) / EPS
    top = jnp.max(score, axis=1, keepdims=True)
    shifted = jnp.exp(score - top)
    probs = shifted.astype(BF16)
    diag = (lax.broadcasted_iota(jnp.int32, (rows, lanes), 0)
            == lax.broadcasted_iota(jnp.int32, (rows, lanes), 1))

    def as_row(column):
        return jnp.sum(jnp.where(diag, column, 0.0), axis=0, keepdims=True)

    for c in range(parts):
        part = jnp.dot(probs, sites_v[:, c * wide:(c + 1) * wide], preferred_element_type=F32)
        for d in range(n):
            t_send[c, d] = part[d * rows_dev:(d + 1) * rows_dev, :].astype(BF16)

        def t_to(k):
            t = other(k)
            to_site(t_send.at[c, t], t_all.at[c, me], ts_sem.at[c], tr_sem.at[c], t)

        steps(n - 1, t_to)
        if c == 0:
            stat_send[0:1, :] = as_row(top)
            stat_send[1:2, :] = as_row(jnp.sum(shifted, axis=1, keepdims=True))
            steps(n - 1, lambda k: to_site(stat_send, stat_all.at[me], ss_sem, sr_sem, other(k)))
            stat_all[me] = stat_send[...]

    drain(stat_all.at[pl.ds(0, n - 1)], sr_sem)
    peak = stat_all[0, 0:1, :]
    for d in range(1, n):
        peak = jnp.maximum(peak, stat_all[d, 0:1, :])
    whole = 0.0
    for d in range(n):
        whole = whole + jnp.exp(stat_all[d, 0:1, :] - peak) * stat_all[d, 1:2, :]
    lse_row = peak + jnp.log(jnp.where(whole > 0.0, whole, 1.0))
    lse = jnp.sum(jnp.where(diag, lse_row, 0.0), axis=1, keepdims=True)
    mass_part = jnp.sum(jnp.exp(score - lse), axis=0, keepdims=True)
    mass_send[...] = mass_part

    def mass_to(k):
        pltpu.make_async_remote_copy(
            src_ref=mass_send, dst_ref=mass_all.at[mg], send_sem=ms_sem, recv_sem=mr_sem,
            device_id={"grp": lax.rem(mg + k + 1, g)}, device_id_type=MESH).start()

    steps(g - 1, mass_to)
    mass_all[mg] = mass_part

    mine_diag = (lax.broadcasted_iota(jnp.int32, (rows_dev, lanes), 0) + me * rows_dev
                 == lax.broadcasted_iota(jnp.int32, (rows_dev, lanes), 1))
    own_lse = jnp.sum(jnp.where(mine_diag, lse_row, 0.0), axis=1, keepdims=True)
    pot = own_sq - EPS * (own_lse - math.log(float(n_loc * n)))
    first = (lax.broadcasted_iota(jnp.int32, (rows_dev, 128), 0)
             == lax.broadcasted_iota(jnp.int32, (rows_dev, 128), 1))
    pot_ref[...] = jnp.sum(jnp.where(first, pot, 0.0), axis=0, keepdims=True)[:, :rows_dev]

    shares = []
    for d in range(n):
        share_row = jnp.exp(stat_all[d, 0:1, :] - lse_row)
        shares.append(jnp.sum(jnp.where(mine_diag, share_row, 0.0), axis=1, keepdims=True))
    for c in range(parts):
        t_all[c, me] = t_send[c, me]
    for c in range(parts):
        drain(t_all.at[c, pl.ds(0, n - 1)], tr_sem.at[c])
        acc = None
        for d in range(n):
            term = shares[d] * t_all[c, d].astype(F32)
            acc = term if acc is None else acc + term
        tgt_ref[:, c * wide:(c + 1) * wide] = acc.astype(BF16)

    drain(mass_all.at[pl.ds(0, g - 1)], mr_sem)
    mass = jnp.sum(mass_all[...], axis=0)
    neww_ref[...] = weights_v[...] + ETA * (1.0 - float(n_loc * n) / float(rows * g) * mass)

    drain(stat_all.at[pl.ds(0, n - 1)], ss_sem)
    for c in range(n_parts):
        drain(noise_all.at[c, pl.ds(0, n - 1)], ns_sem.at[c])
    for c in range(parts):
        drain(t_all.at[c, pl.ds(0, n - 1)], ts_sem.at[c])
    drain(mass_all.at[pl.ds(0, g - 1)], ms_sem)


def place(tgt, pot, neww, tgt_out, pot_out, neww_out, sems):
    copies = [pltpu.make_async_copy(src, dst, sems.at[i])
              for i, (src, dst) in enumerate(((tgt, tgt_out), (pot, pot_out), (neww, neww_out)))]
    for copy in copies:
        copy.start()
    for copy in copies:
        copy.wait()


def shards(n, g, noise, sites, weights):
    rows_dev, width = noise.shape
    n_loc = sites.shape[0]
    rows = rows_dev * n
    lanes = max(128, rows)
    chunks, parts, n_parts = 4, 4, 2
    vmem = pl.BlockSpec(memory_space=pltpu.VMEM)
    anym = pl.BlockSpec(memory_space=pl.ANY)
    dma = pltpu.SemaphoreType.DMA
    tgt, pot, neww = pl.pallas_call(
        functools.partial(kernel, n, g),
        out_shape=(
            pltpu.VMEM((rows_dev, width), BF16),
            pltpu.VMEM((1, rows_dev), F32),
            pltpu.VMEM((1, n_loc), F32),
        ),
        in_specs=[anym, anym, anym],
        out_specs=(vmem, vmem, vmem),
        scratch_shapes=[
            pltpu.VMEM((n_loc, width), BF16),
            pltpu.VMEM((1, n_loc), F32),
            pltpu.VMEM((n_parts, n, rows_dev, width // n_parts), BF16),
            pltpu.VMEM((n_parts, rows, width // n_parts), F32),
            pltpu.VMEM((n_loc, 128), F32),
            pltpu.VMEM((parts, n, rows_dev, width // parts), BF16),
            pltpu.VMEM((parts, n, rows_dev, width // parts), BF16),
            pltpu.VMEM((2, lanes), F32),
            pltpu.VMEM((n, 2, lanes), F32),
            pltpu.VMEM((1, n_loc), F32),
            pltpu.VMEM((g, 1, n_loc), F32),
            dma((chunks,)), dma((2,)), dma((n_parts,)), dma((n_parts,)), dma((parts,)), dma((parts,)),
            dma(()), dma(()), dma(()), dma(()),
        ],
        compiler_params=pltpu.CompilerParams(
            collective_id=0, has_side_effects=True, vmem_limit_bytes=56 * 1024 * 1024),
        name="dual_step",
    )(noise, sites, weights.reshape(1, n_loc))
    outs = (tgt, pot.reshape(rows_dev), neww.reshape(n_loc))
    return pl.pallas_call(
        place,
        out_shape=tuple(jax.ShapeDtypeStruct(o.shape, o.dtype) for o in outs),
        in_specs=[vmem] * 3,
        out_specs=(anym,) * 3,
        scratch_shapes=[dma((3,))],
        compiler_params=pltpu.CompilerParams(vmem_limit_bytes=1024 * 1024),
        name="place",
    )(*outs)


def solution(mesh):
    n, g = mesh.shape["site"], mesh.shape["grp"]
    in_specs = (P(("grp", "site"), None), P("site", None), P("site"))
    out_specs = (P(("grp", "site"), None), P(("grp", "site")), P("site"))
    return jax.shard_map(functools.partial(shards, n, g), mesh=mesh, in_specs=in_specs,
                         out_specs=out_specs, check_vma=False)
```

```python
import functools
import math

import jax
import jax.numpy as jnp
from jax import lax
from jax.experimental import pallas as pl
from jax.experimental.pallas import tpu as pltpu
from jax.sharding import PartitionSpec as P

EPS = 0.006
ETA = 0.05
MESH = pl.DeviceIdType.MESH
F32 = jnp.float32
BF16 = jnp.bfloat16


def steps(count, body):
    if count <= 16:
        for k in range(count):
            body(k)
    else:
        lax.fori_loop(0, count, lambda k, c: (body(k), c)[1], 0)


def kernel(n, g, noise_ref, sites_ref, weights_ref, tgt_ref, pot_ref, neww_ref,
           sites_v, weights_v, noise_all, noise_f, sq_acc, t_send, t_all,
           stat_send, stat_all, mass_send, mass_all,
           site_sem, own_sem, ns_sem, nr_sem, ts_sem, tr_sem, ss_sem, sr_sem, ms_sem, mr_sem):
    me = lax.axis_index("site")
    mg = lax.axis_index("grp")
    rows_dev, width = noise_ref.shape
    n_loc = sites_ref.shape[0]
    rows = rows_dev * n
    lanes = stat_send.shape[1]
    chunks = site_sem.shape[0]
    crow = n_loc // chunks
    parts, wide = t_send.shape[0], t_send.shape[3]

    def site_copy(c):
        part = pl.ds(c * crow, crow)
        return pltpu.make_async_copy(sites_ref.at[part, :], sites_v.at[part, :], site_sem.at[c])

    barrier = pltpu.get_barrier_semaphore()

    def greet_site(k):
        pl.semaphore_signal(barrier, inc=1, device_id={"site": lax.rem(me + k + 1, n)}, device_id_type=MESH)

    def greet_grp(k):
        pl.semaphore_signal(barrier, inc=1, device_id={"grp": lax.rem(mg + k + 1, g)}, device_id_type=MESH)

    steps(n - 1, greet_site)
    steps(g - 1, greet_grp)
    for c in range(chunks):
        site_copy(c).start()
    for c in range(parts):
        pltpu.make_async_copy(noise_ref.at[:, pl.ds(c * wide, wide)], noise_all.at[c, me], own_sem.at[0]).start()
    own_w = pltpu.make_async_copy(weights_ref, weights_v, own_sem.at[1])
    own_w.start()
    pl.semaphore_wait(barrier, n + g - 2)

    def to_site(src, dst, s_sem, r_sem, t):
        pltpu.make_async_remote_copy(
            src_ref=src, dst_ref=dst, send_sem=s_sem, recv_sem=r_sem,
            device_id={"site": t}, device_id_type=MESH).start()

    def drain(blocks, sem):
        pltpu.make_async_copy(blocks, blocks, sem).wait()

    def other(k):
        return lax.rem(me + k + 1, n)

    for c in range(parts):
        steps(n - 1, lambda k: to_site(noise_ref.at[:, pl.ds(c * wide, wide)], noise_all.at[c, me],
                                       ns_sem.at[c], nr_sem.at[c], other(k)))

    for c in range(chunks):
        site_copy(c).wait()
        acc = None
        for j in range(width // 128):
            x = sites_v[c * crow:(c + 1) * crow, j * 128:(j + 1) * 128].astype(F32)
            acc = x * x if acc is None else acc + x * x
        sq_acc[c * crow:(c + 1) * crow, :] = acc
    half_sq = jnp.sum(sq_acc[...].T, axis=0, keepdims=True) / (2.0 * width)
    drain(noise_ref, own_sem.at[0])
    own_w.wait()
    own_sq = 0.0
    for c in range(parts):
        mine = noise_all[c, me].astype(F32)
        own_sq = own_sq + jnp.sum(mine * mine, axis=1, keepdims=True)
    own_sq = own_sq / (2.0 * width)

    inner = None
    for c in range(parts):
        drain(noise_all.at[c, pl.ds(0, n - 1)], nr_sem.at[c])
        for d in range(n):
            noise_f[c, d * rows_dev:(d + 1) * rows_dev, :] = noise_all[c, d].astype(F32)
        term = lax.dot_general(noise_f[c].astype(BF16), sites_v[:, c * wide:(c + 1) * wide],
                               (((1,), (1,)), ((), ())), preferred_element_type=F32)
        inner = term if inner is None else inner + term
    score = weights_v[...] + (inner / width - half_sq) / EPS
    top = jnp.max(score, axis=1, keepdims=True)
    shifted = jnp.exp(score - top)
    total = jnp.sum(shifted, axis=1, keepdims=True)
    lse_d = top + jnp.log(total)

    diag = (lax.broadcasted_iota(jnp.int32, (rows, lanes), 0)
            == lax.broadcasted_iota(jnp.int32, (rows, lanes), 1))
    stat_send[...] = jnp.sum(jnp.where(diag, lse_d, 0.0), axis=0, keepdims=True)
    steps(n - 1, lambda k: to_site(stat_send, stat_all.at[me], ss_sem, sr_sem, other(k)))
    stat_all[me] = stat_send[...]

    probs = shifted.astype(BF16)
    inv = 1.0 / total
    def targets(c):
        part = jnp.dot(probs, sites_v[:, c * wide:(c + 1) * wide], preferred_element_type=F32) * inv
        for d in range(n):
            t_send[c, d] = part[d * rows_dev:(d + 1) * rows_dev, :].astype(BF16)

        def t_to(k):
            t = other(k)
            to_site(t_send.at[c, t], t_all.at[c, me], ts_sem.at[c], tr_sem.at[c], t)

        steps(n - 1, t_to)

    for c in range(parts // 2):
        targets(c)

    drain(stat_all.at[pl.ds(0, n - 1)], sr_sem)
    stats = stat_all[...]
    peak = jnp.max(stats, axis=0)
    lse_row = peak + jnp.log(jnp.sum(jnp.exp(stats - peak[None]), axis=0))
    lse = jnp.sum(jnp.where(diag, lse_row, 0.0), axis=1, keepdims=True)
    mass_part = jnp.sum(jnp.exp(score - lse), axis=0, keepdims=True)
    mass_send[...] = mass_part

    def mass_to(k):
        pltpu.make_async_remote_copy(
            src_ref=mass_send, dst_ref=mass_all.at[mg], send_sem=ms_sem, recv_sem=mr_sem,
            device_id={"grp": lax.rem(mg + k + 1, g)}, device_id_type=MESH).start()

    steps(g - 1, mass_to)
    mass_all[mg] = mass_part

    for c in range(parts // 2, parts):
        targets(c)

    mine_diag = (lax.broadcasted_iota(jnp.int32, (rows_dev, lanes), 0) + me * rows_dev
                 == lax.broadcasted_iota(jnp.int32, (rows_dev, lanes), 1))
    own_lse = jnp.sum(jnp.where(mine_diag, lse_row, 0.0), axis=1, keepdims=True)
    pot = own_sq - EPS * (own_lse - math.log(float(n_loc * n)))
    first = (lax.broadcasted_iota(jnp.int32, (rows_dev, 128), 0)
             == lax.broadcasted_iota(jnp.int32, (rows_dev, 128), 1))
    pot_ref[...] = jnp.sum(jnp.where(first, pot, 0.0), axis=0, keepdims=True)[:, :rows_dev]

    shares = []
    for d in range(n):
        share_row = jnp.exp(stat_all[d] - lse_row)
        shares.append(jnp.sum(jnp.where(mine_diag, share_row, 0.0), axis=1, keepdims=True))
    for c in range(parts):
        t_all[c, me] = t_send[c, me]
    for c in range(parts):
        drain(t_all.at[c, pl.ds(0, n - 1)], tr_sem.at[c])
        acc = None
        for d in range(n):
            term = shares[d] * t_all[c, d].astype(F32)
            acc = term if acc is None else acc + term
        tgt_ref[:, c * wide:(c + 1) * wide] = acc.astype(BF16)

    drain(mass_all.at[pl.ds(0, g - 1)], mr_sem)
    mass = jnp.sum(mass_all[...], axis=0)
    neww_ref[...] = weights_v[...] + ETA * (1.0 - float(n_loc * n) / float(rows * g) * mass)

    drain(stat_all.at[pl.ds(0, n - 1)], ss_sem)
    for c in range(parts):
        drain(noise_all.at[c, pl.ds(0, n - 1)], ns_sem.at[c])
        drain(t_all.at[c, pl.ds(0, n - 1)], ts_sem.at[c])
    drain(mass_all.at[pl.ds(0, g - 1)], ms_sem)


def place(tgt, pot, neww, tgt_out, pot_out, neww_out, sems):
    copies = [pltpu.make_async_copy(src, dst, sems.at[i])
              for i, (src, dst) in enumerate(((tgt, tgt_out), (pot, pot_out), (neww, neww_out)))]
    for copy in copies:
        copy.start()
    for copy in copies:
        copy.wait()


def shards(n, g, noise, sites, weights):
    rows_dev, width = noise.shape
    n_loc = sites.shape[0]
    rows = rows_dev * n
    lanes = max(128, rows)
    chunks, parts = 8, 4
    vmem = pl.BlockSpec(memory_space=pltpu.VMEM)
    anym = pl.BlockSpec(memory_space=pl.ANY)
    dma = pltpu.SemaphoreType.DMA
    tgt, pot, neww = pl.pallas_call(
        functools.partial(kernel, n, g),
        out_shape=(
            pltpu.VMEM((rows_dev, width), BF16),
            pltpu.VMEM((1, rows_dev), F32),
            pltpu.VMEM((1, n_loc), F32),
        ),
        in_specs=[anym, anym, anym],
        out_specs=(vmem, vmem, vmem),
        scratch_shapes=[
            pltpu.VMEM((n_loc, width), BF16),
            pltpu.VMEM((1, n_loc), F32),
            pltpu.VMEM((parts, n, rows_dev, width // parts), BF16),
            pltpu.VMEM((parts, rows, width // parts), F32),
            pltpu.VMEM((n_loc, 128), F32),
            pltpu.VMEM((parts, n, rows_dev, width // parts), BF16),
            pltpu.VMEM((parts, n, rows_dev, width // parts), BF16),
            pltpu.VMEM((1, lanes), F32),
            pltpu.VMEM((n, 1, lanes), F32),
            pltpu.VMEM((1, n_loc), F32),
            pltpu.VMEM((g, 1, n_loc), F32),
            dma((chunks,)), dma((2,)), dma((parts,)), dma((parts,)), dma((parts,)), dma((parts,)),
            dma(()), dma(()), dma(()), dma(()),
        ],
        compiler_params=pltpu.CompilerParams(
            collective_id=0, has_side_effects=True, vmem_limit_bytes=56 * 1024 * 1024),
        name="dual_step",
    )(noise, sites, weights.reshape(1, n_loc))
    outs = (tgt, pot.reshape(rows_dev), neww.reshape(n_loc))
    return pl.pallas_call(
        place,
        out_shape=tuple(jax.ShapeDtypeStruct(o.shape, o.dtype) for o in outs),
        in_specs=[vmem] * 3,
        out_specs=(anym,) * 3,
        scratch_shapes=[dma((3,))],
        compiler_params=pltpu.CompilerParams(vmem_limit_bytes=1024 * 1024),
        name="place",
    )(*outs)


def solution(mesh):
    n, g = mesh.shape["site"], mesh.shape["grp"]
    in_specs = (P(("grp", "site"), None), P("site", None), P("site"))
    out_specs = (P(("grp", "site"), None), P(("grp", "site")), P("site"))
    return jax.shard_map(functools.partial(shards, n, g), mesh=mesh, in_specs=in_specs,
                         out_specs=out_specs, check_vma=False)
```

```python
import functools
import math

import jax
import jax.numpy as jnp
from jax import lax
from jax.experimental import pallas as pl
from jax.experimental.pallas import tpu as pltpu
from jax.sharding import PartitionSpec as P

EPS = 0.006
ETA = 0.05
MESH = pl.DeviceIdType.MESH
F32 = jnp.float32
BF16 = jnp.bfloat16


def steps(count, body):
    if count <= 16:
        for k in range(count):
            body(k)
    else:
        lax.fori_loop(0, count, lambda k, c: (body(k), c)[1], 0)


def kernel(n, g, noise_ref, sites_ref, weights_ref, tgt_ref, pot_ref, neww_ref,
           sites_v, weights_v, noise_all, noise_f, sq_acc, t_send, t_all,
           stat_send, stat_all, mass_send, mass_all,
           site_sem, own_sem, ns_sem, nr_sem, ts_sem, tr_sem, ss_sem, sr_sem, ms_sem, mr_sem):
    me = lax.axis_index("site")
    mg = lax.axis_index("grp")
    rows_dev, width = noise_ref.shape
    n_loc = sites_ref.shape[0]
    rows = rows_dev * n
    lanes = stat_send.shape[1]
    chunks = site_sem.shape[0]
    crow = n_loc // chunks
    parts, wide = t_send.shape[0], t_send.shape[3]
    n_parts, n_wide = noise_all.shape[0], noise_all.shape[3]

    def site_copy(c):
        part = pl.ds(c * crow, crow)
        return pltpu.make_async_copy(sites_ref.at[part, :], sites_v.at[part, :], site_sem.at[c])

    barrier = pltpu.get_barrier_semaphore()

    def greet_site(k):
        pl.semaphore_signal(barrier, inc=1, device_id={"site": lax.rem(me + k + 1, n)}, device_id_type=MESH)

    def greet_grp(k):
        pl.semaphore_signal(barrier, inc=1, device_id={"grp": lax.rem(mg + k + 1, g)}, device_id_type=MESH)

    steps(n - 1, greet_site)
    steps(g - 1, greet_grp)
    for c in range(chunks):
        site_copy(c).start()
    for c in range(n_parts):
        pltpu.make_async_copy(noise_ref.at[:, pl.ds(c * n_wide, n_wide)], noise_all.at[c, me], own_sem.at[0]).start()
    own_w = pltpu.make_async_copy(weights_ref, weights_v, own_sem.at[1])
    own_w.start()
    pl.semaphore_wait(barrier, n + g - 2)

    def to_site(src, dst, s_sem, r_sem, t):
        pltpu.make_async_remote_copy(
            src_ref=src, dst_ref=dst, send_sem=s_sem, recv_sem=r_sem,
            device_id={"site": t}, device_id_type=MESH).start()

    def drain(blocks, sem):
        pltpu.make_async_copy(blocks, blocks, sem).wait()

    def other(k):
        return lax.rem(me + k + 1, n)

    for c in range(n_parts):
        steps(n - 1, lambda k: to_site(noise_ref.at[:, pl.ds(c * n_wide, n_wide)], noise_all.at[c, me],
                                       ns_sem.at[c], nr_sem.at[c], other(k)))

    for c in range(chunks):
        site_copy(c).wait()
        acc = None
        for j in range(width // 128):
            x = sites_v[c * crow:(c + 1) * crow, j * 128:(j + 1) * 128].astype(F32)
            acc = x * x if acc is None else acc + x * x
        sq_acc[c * crow:(c + 1) * crow, :] = acc
    half_sq = jnp.sum(sq_acc[...].T, axis=0, keepdims=True) / (2.0 * width)
    drain(noise_ref, own_sem.at[0])
    own_w.wait()
    own_sq = 0.0
    for c in range(n_parts):
        mine = noise_all[c, me].astype(F32)
        own_sq = own_sq + jnp.sum(mine * mine, axis=1, keepdims=True)
    own_sq = own_sq / (2.0 * width)

    inner = None
    for c in range(n_parts):
        drain(noise_all.at[c, pl.ds(0, n - 1)], nr_sem.at[c])
        for d in range(n):
            noise_f[c, d * rows_dev:(d + 1) * rows_dev, :] = noise_all[c, d].astype(F32)
        term = lax.dot_general(noise_f[c].astype(BF16), sites_v[:, c * n_wide:(c + 1) * n_wide],
                               (((1,), (1,)), ((), ())), preferred_element_type=F32)
        inner = term if inner is None else inner + term
    score = weights_v[...] + (inner / width - half_sq) / EPS
    top = jnp.max(score, axis=1, keepdims=True)
    shifted = jnp.exp(score - top)
    probs = shifted.astype(BF16)
    diag = (lax.broadcasted_iota(jnp.int32, (rows, lanes), 0)
            == lax.broadcasted_iota(jnp.int32, (rows, lanes), 1))

    def as_row(column):
        return jnp.sum(jnp.where(diag, column, 0.0), axis=0, keepdims=True)

    for c in range(parts):
        part = jnp.dot(probs, sites_v[:, c * wide:(c + 1) * wide], preferred_element_type=F32)
        for d in range(n):
            t_send[c, d] = part[d * rows_dev:(d + 1) * rows_dev, :].astype(BF16)

        def t_to(k):
            t = other(k)
            to_site(t_send.at[c, t], t_all.at[c, me], ts_sem.at[c], tr_sem.at[c], t)

        steps(n - 1, t_to)
        if c == 0:
            stat_send[0:1, :] = as_row(top)
            stat_send[1:2, :] = as_row(jnp.sum(shifted, axis=1, keepdims=True))
            steps(n - 1, lambda k: to_site(stat_send, stat_all.at[me], ss_sem, sr_sem, other(k)))
            stat_all[me] = stat_send[...]

    drain(stat_all.at[pl.ds(0, n - 1)], sr_sem)
    peak = stat_all[0, 0:1, :]
    for d in range(1, n):
        peak = jnp.maximum(peak, stat_all[d, 0:1, :])
    whole = 0.0
    for d in range(n):
        whole = whole + jnp.exp(stat_all[d, 0:1, :] - peak) * stat_all[d, 1:2, :]
    lse_row = peak + jnp.log(jnp.where(whole > 0.0, whole, 1.0))
    lse = jnp.sum(jnp.where(diag, lse_row, 0.0), axis=1, keepdims=True)
    mass_part = jnp.sum(jnp.exp(score - lse), axis=0, keepdims=True)
    mass_send[...] = mass_part

    def mass_to(k):
        pltpu.make_async_remote_copy(
            src_ref=mass_send, dst_ref=mass_all.at[mg], send_sem=ms_sem, recv_sem=mr_sem,
            device_id={"grp": lax.rem(mg + k + 1, g)}, device_id_type=MESH).start()

    steps(g - 1, mass_to)
    mass_all[mg] = mass_part

    mine_diag = (lax.broadcasted_iota(jnp.int32, (rows_dev, lanes), 0) + me * rows_dev
                 == lax.broadcasted_iota(jnp.int32, (rows_dev, lanes), 1))
    own_lse = jnp.sum(jnp.where(mine_diag, lse_row, 0.0), axis=1, keepdims=True)
    pot = own_sq - EPS * (own_lse - math.log(float(n_loc * n)))
    first = (lax.broadcasted_iota(jnp.int32, (rows_dev, 128), 0)
             == lax.broadcasted_iota(jnp.int32, (rows_dev, 128), 1))
    pot_ref[...] = jnp.sum(jnp.where(first, pot, 0.0), axis=0, keepdims=True)[:, :rows_dev]

    shares = []
    for d in range(n):
        share_row = jnp.exp(stat_all[d, 0:1, :] - lse_row)
        shares.append(jnp.sum(jnp.where(mine_diag, share_row, 0.0), axis=1, keepdims=True))
    for c in range(parts):
        t_all[c, me] = t_send[c, me]
    for c in range(parts):
        drain(t_all.at[c, pl.ds(0, n - 1)], tr_sem.at[c])
        acc = None
        for d in range(n):
            term = shares[d] * t_all[c, d].astype(F32)
            acc = term if acc is None else acc + term
        tgt_ref[:, c * wide:(c + 1) * wide] = acc.astype(BF16)

    drain(mass_all.at[pl.ds(0, g - 1)], mr_sem)
    mass = jnp.sum(mass_all[...], axis=0)
    neww_ref[...] = weights_v[...] + ETA * (1.0 - float(n_loc * n) / float(rows * g) * mass)

    drain(stat_all.at[pl.ds(0, n - 1)], ss_sem)
    for c in range(n_parts):
        drain(noise_all.at[c, pl.ds(0, n - 1)], ns_sem.at[c])
    for c in range(parts):
        drain(t_all.at[c, pl.ds(0, n - 1)], ts_sem.at[c])
    drain(mass_all.at[pl.ds(0, g - 1)], ms_sem)


def place(tgt, pot, neww, tgt_out, pot_out, neww_out, sems):
    copies = [pltpu.make_async_copy(src, dst, sems.at[i])
              for i, (src, dst) in enumerate(((tgt, tgt_out), (pot, pot_out), (neww, neww_out)))]
    for copy in copies:
        copy.start()
    for copy in copies:
        copy.wait()


def shards(n, g, noise, sites, weights):
    rows_dev, width = noise.shape
    n_loc = sites.shape[0]
    rows = rows_dev * n
    lanes = max(128, rows)
    chunks, parts, n_parts = 8, 4, 4
    vmem = pl.BlockSpec(memory_space=pltpu.VMEM)
    anym = pl.BlockSpec(memory_space=pl.ANY)
    dma = pltpu.SemaphoreType.DMA
    tgt, pot, neww = pl.pallas_call(
        functools.partial(kernel, n, g),
        out_shape=(
            pltpu.VMEM((rows_dev, width), BF16),
            pltpu.VMEM((1, rows_dev), F32),
            pltpu.VMEM((1, n_loc), F32),
        ),
        in_specs=[anym, anym, anym],
        out_specs=(vmem, vmem, vmem),
        scratch_shapes=[
            pltpu.VMEM((n_loc, width), BF16),
            pltpu.VMEM((1, n_loc), F32),
            pltpu.VMEM((n_parts, n, rows_dev, width // n_parts), BF16),
            pltpu.VMEM((n_parts, rows, width // n_parts), F32),
            pltpu.VMEM((n_loc, 128), F32),
            pltpu.VMEM((parts, n, rows_dev, width // parts), BF16),
            pltpu.VMEM((parts, n, rows_dev, width // parts), BF16),
            pltpu.VMEM((2, lanes), F32),
            pltpu.VMEM((n, 2, lanes), F32),
            pltpu.VMEM((1, n_loc), F32),
            pltpu.VMEM((g, 1, n_loc), F32),
            dma((chunks,)), dma((2,)), dma((n_parts,)), dma((n_parts,)), dma((parts,)), dma((parts,)),
            dma(()), dma(()), dma(()), dma(()),
        ],
        compiler_params=pltpu.CompilerParams(
            collective_id=0, has_side_effects=True, vmem_limit_bytes=56 * 1024 * 1024),
        name="dual_step",
    )(noise, sites, weights.reshape(1, n_loc))
    outs = (tgt, pot.reshape(rows_dev), neww.reshape(n_loc))
    return pl.pallas_call(
        place,
        out_shape=tuple(jax.ShapeDtypeStruct(o.shape, o.dtype) for o in outs),
        in_specs=[vmem] * 3,
        out_specs=(anym,) * 3,
        scratch_shapes=[dma((3,))],
        compiler_params=pltpu.CompilerParams(vmem_limit_bytes=1024 * 1024),
        name="place",
    )(*outs)


def solution(mesh):
    n, g = mesh.shape["site"], mesh.shape["grp"]
    in_specs = (P(("grp", "site"), None), P("site", None), P("site"))
    out_specs = (P(("grp", "site"), None), P(("grp", "site")), P("site"))
    return jax.shard_map(functools.partial(shards, n, g), mesh=mesh, in_specs=in_specs,
                         out_specs=out_specs, check_vma=False)
```
